128 devices in a mesh: inner: 16 (over x, z_lo, core), outer: 8 (over z_hi, y).
Axes of the slice: x: 4, y: 4, z: 4 (z_hi: 2, z_lo: 2; z = z_hi * 2 + z_lo), core: 2. Of those that a mesh axis runs over, the one named last changes fastest.
Arguments:
- queries: bfloat16 [16384, 1024], P(('inner', 'outer')), may hold values from -8 to 8
- keys: bfloat16 [16384, 128], P(('inner', 'outer')), may hold values from -8 to 8
- values: bfloat16 [16384, 128], P(('inner', 'outer')), may hold values from -6 to 6
- outputs: bfloat16 [16384, 1024], P(('inner', 'outer')), may hold values from -6 to 6
- out_grad: bfloat16 [16384, 1024], P(('inner', 'outer')), may hold values from -6 to 6
- block_order: int32 [256], replicated, may hold values from 0 to 255, each once
Outputs:
- query_grad: bfloat16 [16384, 1024], P(('inner', 'outer'))
- key_grad: float32 [16384, 128], P(('inner', 'outer'))
- value_grad: float32 [16384, 128], P(('inner', 'outer'))
The draws below stay inside these ranges and needn't reach their ends.
Inputs may be any that keep to these rules, and one draw needn't show every extreme that they name: `block_order`: each block number appears once.
All inputs are finite; a program needn't handle non-finite values.
Results may differ from the reference program's by a relative error of at most 0.015.
Values may be sent and summed in bfloat16 or wider, within the bound.
No kernel may reach another device: no remote copies, remote signals or barrier semaphores. Data moves between devices by JAX's collectives and lax.ppermute only.
A program may use at most 128 MiB of HBM per device.

```python
import math
import jax
import jax.numpy as jnp
from jax import lax

DH = 128
HEADS = 8
BLOCK = 64
NBLK = 256
TOKENS = 16384


def draw_queries(key, part):
    key = jax.random.fold_in(key, 11)
    base = jnp.clip(jax.random.normal(key, (TOKENS, HEADS * DH), jnp.float32), -6.0, 6.0)
    return base.astype(jnp.bfloat16)


def draw_keys(key, part):
    key = jax.random.fold_in(key, 23)
    base = jnp.clip(jax.random.normal(key, (TOKENS, DH), jnp.float32), -6.0, 6.0)
    return base.astype(jnp.bfloat16)


def steps_of(key, shape, pieces, low, largest):
    def one(dim, blocks):
        steps = jax.random.uniform(jax.random.fold_in(jax.random.fold_in(key, 6), dim), (blocks,), jnp.float32, low / len(pieces), largest / len(pieces))
        return jnp.repeat(jnp.exp(steps), shape[dim] // blocks).reshape((-1,) + (1,) * (len(shape) - dim - 1))

    loudness = one(*pieces[0])
    for cut in pieces[1:]:
        loudness = loudness * one(*cut)
    return loudness


def centred(stream_key, shape, spread, most, cuts=(), held_as=jnp.bfloat16):
    array = jax.random.normal(stream_key, shape, jnp.float32) * spread
    if len(cuts) > 0:
        array = steps_of(stream_key, shape, cuts, -0.22, 0.18) * array
    return jnp.clip(array, min=-most, max=most).astype(held_as)


def setup_inputs(seed: int = 0) -> dict:
    key_list = jax.random.split(jax.random.key(seed), 7)
    queries = draw_queries(jax.random.fold_in(key_list[6], 71), 0)
    keys = draw_keys(jax.random.fold_in(key_list[6], 71), 0)
    values = centred(key_list[2], (TOKENS, DH), 1.0, 6.0, ((0, 128),))
    outputs = centred(key_list[3], (TOKENS, HEADS * DH), 1.0, 6.0, ((0, 128),))
    out_grad = centred(key_list[4], (TOKENS, HEADS * DH), 1.0, 6.0, ((0, 128),))
    block_order = jax.random.permutation(key_list[5], NBLK).astype(jnp.int32)
    return dict(queries=queries, keys=keys, values=values, outputs=outputs, out_grad=out_grad, block_order=block_order)


def reference(queries, keys, values, outputs, out_grad, block_order):
    scale = DH ** -0.5
    position = jnp.repeat(block_order, BLOCK) * BLOCK + jnp.tile(jnp.arange(BLOCK, dtype=jnp.int32), NBLK)
    query_rows = queries.reshape(TOKENS, HEADS, DH)
    grad_rows = out_grad.reshape(TOKENS, HEADS, DH)
    out_rows = outputs.reshape(TOKENS, HEADS, DH)
    delta = jnp.sum(grad_rows.astype(jnp.float32) * out_rows.astype(jnp.float32), axis=2)
    key_full = keys.astype(jnp.float32)
    value_full = values.astype(jnp.float32)
    qblock = math.gcd(TOKENS, 512)
    steps_count = TOKENS // qblock

    def step(carry, index):
        key_acc, value_acc = carry
        start = (index * qblock).astype(jnp.int32)
        qpart = lax.dynamic_slice_in_dim(query_rows, start, qblock, 0).astype(jnp.float32)
        gpart = lax.dynamic_slice_in_dim(grad_rows, start, qblock, 0).astype(jnp.float32)
        dpart = lax.dynamic_slice_in_dim(delta, start, qblock, 0)
        ppart = lax.dynamic_slice_in_dim(position, start, qblock, 0)
        scores = jnp.einsum('qhd,kd->qhk', qpart, key_full) * scale
        visible = position[None, None, :] <= ppart[:, None, None]
        scores = jnp.where(visible, scores, -jnp.inf)
        top = jnp.max(scores, axis=2, keepdims=True)
        lse = top + jnp.log(jnp.sum(jnp.exp(scores - top), axis=2, keepdims=True))
        prob = jnp.exp(scores - lse)
        probs = prob.astype(jnp.bfloat16)
        dprob = jnp.einsum('qhd,kd->qhk', gpart, value_full)
        grads = (prob * (dprob - dpart[:, :, None]) * scale).astype(jnp.bfloat16)
        query_part = jnp.einsum('qhk,kd->qhd', grads.astype(jnp.float32), key_full).astype(jnp.bfloat16)
        key_acc = key_acc + jnp.einsum('qhk,qhd->kd', grads.astype(jnp.float32), qpart)
        value_acc = value_acc + jnp.einsum('qhk,qhd->kd', probs.astype(jnp.float32), gpart)
        return (key_acc, value_acc), query_part

    start_acc = (jnp.zeros((TOKENS, DH), jnp.float32), jnp.zeros((TOKENS, DH), jnp.float32))
    (key_grad, value_grad), query_parts = lax.scan(step, start_acc, jnp.arange(steps_count, dtype=jnp.int32))
    query_grad = query_parts.reshape(TOKENS, HEADS * DH)
    return query_grad, key_grad, value_grad
```

```python
import functools
import math

import jax
import jax.numpy as jnp
from jax import lax
from jax.experimental import pallas as pl
from jax.experimental.pallas import tpu as pltpu
from jax.sharding import Mesh, PartitionSpec as P

DH = 128
HEADS = 8
BLOCK = 64
ROWS = HEADS * BLOCK
SCALE = DH ** -0.5
C2 = SCALE * math.log2(math.e)
NEG = -1e30
KB = 8
KT = KB * BLOCK
VMEM_LIMIT = 56 * 1024 * 1024
F32 = jnp.float32
BF16 = jnp.bfloat16
KEY_AXES = ("x", "zl", "zh")


def nn(a, b):
    return lax.dot_general(a, b, (((1,), (0,)), ((), ())), preferred_element_type=F32)


def sort_blocks(rank_ref, src, dst, nk):
    def body(j, c):
        r = pl.multiple_of(rank_ref[j] * BLOCK, BLOCK)
        dst[pl.ds(r, BLOCK), :] = src[pl.ds(pl.multiple_of(j * BLOCK, BLOCK), BLOCK), :]
        return c

    lax.fori_loop(0, nk, body, 0)


def causal(s, place_ref, t, query_place, diff):
    parts = []
    for u in range(KB):
        place = place_ref[t * KB + u]
        limit = jnp.where(place < query_place, BLOCK, jnp.where(place == query_place, 0, -2 * BLOCK))
        parts.append(jnp.where(diff <= limit, s[u * BLOCK:(u + 1) * BLOCK], 2 * NEG))
    return jnp.concatenate(parts, 0)


def difference():
    key = lax.broadcasted_iota(jnp.int32, (BLOCK, ROWS), 0)
    query = lax.broadcasted_iota(jnp.int32, (BLOCK, ROWS), 1) % BLOCK
    return key - query


def for_tiles(n, tile):
    whole = jnp.maximum(n - 1, 0) // KB

    def step(t, c):
        tile(t, False)
        return c

    lax.fori_loop(0, whole, step, 0)

    @pl.when(n > 0)
    def _():
        tile(whole, True)


def lse_kernel(nq, nk, rank_ref, place_ref, n_ref, qp_ref, qg_ref, k_ref, lse_ref, ks, m8, l8):
    sort_blocks(rank_ref, k_ref, ks, nk)

    def block(b, c):
        m8[...] = jnp.full_like(m8, NEG)
        l8[...] = jnp.zeros_like(l8)

        def tile(t, last):
            keys = ks[pl.ds(pl.multiple_of(t * KT, KT), KT), :]
            s = nn(keys, qg_ref[b, :DH, :]) * C2
            if last:
                s = causal(s, place_ref, t, qp_ref[b], difference())
            s = s.reshape(KT // 8, 8, ROWS)
            m = m8[...]
            top = jnp.maximum(m, jnp.max(s, axis=0))
            l8[...] = l8[...] * jnp.exp2(m - top) + jnp.sum(jnp.exp2(s - top[None]), axis=0)
            m8[...] = top

        for_tiles(n_ref[b], tile)
        m = m8[...]
        top = jnp.max(m, axis=0, keepdims=True)
        total = jnp.sum(l8[...] * jnp.exp2(m - top), axis=0, keepdims=True)
        lse_ref[b] = jnp.where(total > 0, top + jnp.log2(jnp.maximum(total, 1e-37)), NEG)
        return c

    lax.fori_loop(0, nq, block, 0)


def local_lse(scalars, qg, keys):
    nq = qg.shape[0]
    count = keys.shape[0]
    smem = pl.BlockSpec(memory_space=pltpu.SMEM)
    vmem = pl.BlockSpec(memory_space=pltpu.VMEM)
    return pl.pallas_call(
        functools.partial(lse_kernel, nq, count // BLOCK),
        out_shape=jax.ShapeDtypeStruct((nq, 1, ROWS), F32),
        in_specs=[smem] * 4 + [vmem] * 2,
        out_specs=vmem,
        scratch_shapes=[
            pltpu.VMEM((count, DH), BF16),
            pltpu.VMEM((8, ROWS), F32),
            pltpu.VMEM((8, ROWS), F32),
        ],
        compiler_params=pltpu.CompilerParams(vmem_limit_bytes=VMEM_LIMIT),
        name="local_lse",
    )(*scalars, qg, keys)


def grad_kernel(
    nq, nk, rank_ref, place_ref, n_ref, qp_ref, qg_ref, lse_ref, k_ref, v_ref,
    dq_ref, dkv_ref, ks, vs, kst, dka, dva, dqa, qn, gn,
):
    sort_blocks(rank_ref, k_ref, ks, nk)
    sort_blocks(rank_ref, v_ref, vs, nk)
    kst[...] = ks[...].T
    dka[...] = jnp.zeros_like(dka)
    dva[...] = jnp.zeros_like(dva)

    def block(b, c):
        dqa[...] = jnp.zeros_like(dqa)
        qn[...] = qg_ref[b, :DH, :].T
        gn[...] = qg_ref[b, DH:2 * DH, :].T
        lse = lse_ref[b]
        delta = qg_ref[b, 2 * DH:, :].astype(F32)
        delta = delta[0:1] + delta[1:2] + delta[2:3]

        def tile(t, last):
            at = pl.ds(pl.multiple_of(t * KT, KT), KT)
            s = nn(ks[at, :], qg_ref[b, :DH, :]) * C2 - lse
            if last:
                s = causal(s, place_ref, t, qp_ref[b], difference())
            p = jnp.exp2(s)
            dp = nn(vs[at, :], qg_ref[b, DH:2 * DH, :])
            ds = (p * (dp - delta)).astype(BF16)
            dqa[...] += nn(kst[:, at], ds)
            dva[at, :] += nn(p.astype(BF16), gn[...])
            dka[at, :] += nn(ds, qn[...])

        for_tiles(n_ref[b], tile)
        dq_ref[b] = dqa[...] * SCALE
        return c

    lax.fori_loop(0, nq, block, 0)

    def body(j, c):
        r = pl.ds(pl.multiple_of(rank_ref[j] * BLOCK, BLOCK), BLOCK)
        at = pl.ds(pl.multiple_of(j * BLOCK, BLOCK), BLOCK)
        dkv_ref[at, :DH] = (dka[r, :] * SCALE).astype(dkv_ref.dtype)
        dkv_ref[at, DH:] = dva[r, :].astype(dkv_ref.dtype)
        return c

    lax.fori_loop(0, nk, body, 0)


def local_grads(scalars, qg, lse, keys, values):
    nq = qg.shape[0]
    count = keys.shape[0]
    smem = pl.BlockSpec(memory_space=pltpu.SMEM)
    vmem = pl.BlockSpec(memory_space=pltpu.VMEM)
    return pl.pallas_call(
        functools.partial(grad_kernel, nq, count // BLOCK),
        out_shape=(
            jax.ShapeDtypeStruct((nq, DH, ROWS), F32),
            jax.ShapeDtypeStruct((count, 2 * DH), BF16),
        ),
        in_specs=[smem] * 4 + [vmem] * 4,
        out_specs=(vmem, vmem),
        scratch_shapes=[
            pltpu.VMEM((count, DH), BF16),
            pltpu.VMEM((count, DH), BF16),
            pltpu.VMEM((DH, count), BF16),
            pltpu.VMEM((count, DH), F32),
            pltpu.VMEM((count, DH), F32),
            pltpu.VMEM((DH, ROWS), F32),
            pltpu.VMEM((ROWS, DH), BF16),
            pltpu.VMEM((ROWS, DH), BF16),
        ],
        compiler_params=pltpu.CompilerParams(vmem_limit_bytes=VMEM_LIMIT),
        name="local_grads",
    )(*scalars, qg, lse, keys, values)


def along(axis, shift, size, array):
    return lax.ppermute(array, axis, [(i, (i + shift) % size) for i in range(size)])


def combine(parts):
    top = functools.reduce(jnp.maximum, parts)
    return top + jnp.log2(sum(jnp.exp2(part - top) for part in parts))


def shards(queries, keys, values, outputs, out_grad, block_order):
    y = lax.axis_index("y")
    core = lax.axis_index("core")

    def columns(a):
        return a.reshape(2, BLOCK, HEADS, DH).transpose(0, 3, 2, 1).reshape(2, DH, ROWS)

    product = out_grad.astype(F32) * outputs.astype(F32)
    delta = jnp.sum(product.reshape(2, BLOCK, HEADS, DH), axis=3).transpose(0, 2, 1).reshape(2, 1, ROWS)
    d1 = lax.reduce_precision(delta, 8, 7)
    d2 = lax.reduce_precision(delta - d1, 8, 7)
    d3 = delta - d1 - d2
    extra = jnp.concatenate([d1, d2, d3, jnp.zeros((2, 13, ROWS), F32)], axis=1).astype(BF16)
    own = jnp.concatenate([columns(queries), columns(out_grad), extra], axis=1)

    pair = jnp.concatenate([keys, values], axis=1)
    gathered = lax.all_to_all(jnp.tile(pair, (16, 1)), KEY_AXES, 0, 0, tiled=True)
    key_all, value_all = gathered[:, :DH], gathered[:, DH:]

    pieces = [own] + [along("y", s, 4, own) for s in (1, 2, 3)]
    mine = jnp.stack(pieces)
    other = along("core", 1, 2, mine)
    qg = jnp.stack([mine, other], axis=1).reshape(16, 2 * DH + 16, ROWS)

    order = block_order.reshape(4, 2, 2, 2, 4, 2)
    key_place = lax.dynamic_slice(order, (0, 0, core, 0, y, 0), (4, 2, 1, 2, 1, 2)).reshape(32)
    here = lax.dynamic_slice(
        order, (lax.axis_index("x"), lax.axis_index("zl"), 0, lax.axis_index("zh"), 0, 0), (1, 1, 2, 1, 4, 2)
    ).reshape(2, 4, 2)
    query_place = jnp.stack(
        [jnp.stack([here[core ^ c, (y - s) % 4] for c in range(2)]) for s in range(4)]
    ).reshape(16)
    before = key_place[:, None] < key_place[None, :]
    rank = jnp.sum(before, axis=0, dtype=jnp.int32)
    spots = lax.broadcasted_iota(jnp.int32, (32, 32), 0)
    place = jnp.sum(jnp.where(rank[None, :] == spots, key_place[None, :], 0), axis=1, dtype=jnp.int32)
    visible = jnp.sum(key_place[None, :] <= query_place[:, None], axis=1, dtype=jnp.int32)
    scalars = (rank, place, visible, query_place)

    part = local_lse(scalars, qg, key_all).reshape(4, 2, 2, ROWS)
    part = combine([part, along("core", 1, 2, part)[:, ::-1]])
    around = [part]
    for d in (1, 2, 3):
        peer = along("y", -d, 4, part)
        around.append(jnp.roll(peer, -d, axis=0))
    lse = combine(around).reshape(16, 1, ROWS)

    query_part, kv_part = local_grads(scalars, qg, lse, key_all, value_all)

    query_part = query_part.reshape(4, 2, 2, DH, ROWS)
    query_sum = query_part[:, 0] + along("core", 1, 2, query_part[:, 1])
    total = query_sum[0]
    for s in (1, 2, 3):
        total = total + along("y", -s, 4, query_sum[s].astype(BF16)).astype(F32)
    query_grad = total.astype(BF16).reshape(2, DH, HEADS, BLOCK).transpose(0, 3, 2, 1).reshape(2 * BLOCK, HEADS * DH)

    terms = lax.all_to_all(kv_part, KEY_AXES, 0, 0, tiled=True)
    kv_grad = jnp.sum(terms.astype(F32).reshape(16, 2 * BLOCK, 2 * DH), axis=0)
    return query_grad, kv_grad[:, :DH], kv_grad[:, DH:]


def solution(mesh):
    fine = Mesh(mesh.devices.reshape(4, 2, 2, 2, 4), ("x", "zl", "core", "zh", "y"))
    rows = P(("x", "zl", "core", "zh", "y"), None)
    return jax.shard_map(
        shards,
        mesh=fine,
        in_specs=(rows,) * 5 + (P(),),
        out_specs=(rows,) * 3,
        check_vma=False,
    )
```

```python
import functools
import math

import jax
import jax.numpy as jnp
from jax import lax
from jax.experimental import pallas as pl
from jax.experimental.pallas import tpu as pltpu
from jax.sharding import Mesh, PartitionSpec as P

DH = 128
HEADS = 8
BLOCK = 64
ROWS = HEADS * BLOCK
MESSAGE = 2 * ROWS + 16
SCALE = DH ** -0.5
C2 = SCALE * math.log2(math.e)
NEG = -1e30
KB = 4
KT = KB * BLOCK
UNROLL = 4
HALVES = 1
VMEM_LIMIT = 56 * 1024 * 1024
F32 = jnp.float32
BF16 = jnp.bfloat16
KEY_AXES = ("x", "zl", "zh")
SMEM = pl.BlockSpec(memory_space=pltpu.SMEM)
VMEM = pl.BlockSpec(memory_space=pltpu.VMEM)


def nn(a, b):
    return lax.dot_general(a, b, (((1,), (0,)), ((), ())), preferred_element_type=F32)


def nt(a, b):
    return lax.dot_general(a, b, (((1,), (1,)), ((), ())), preferred_element_type=F32)


def params():
    return pltpu.CompilerParams(vmem_limit_bytes=VMEM_LIMIT)


def cost(products, nq, count):
    area = nq * ROWS * count // 2
    return pl.CostEstimate(flops=products * 4 * area * DH, bytes_accessed=8 << 20, transcendentals=area)


def message_kernel(q_ref, g_ref, o_ref, *out_refs):
    for blk in range(2):
        out_ref, at = out_refs[blk * HALVES // 2], blk % (2 // HALVES)
        tokens = slice(blk * BLOCK, (blk + 1) * BLOCK)
        parts = []
        for h in range(HEADS):
            lanes = slice(h * DH, (h + 1) * DH)
            g = g_ref[tokens, lanes]
            out_ref[at, h * BLOCK:(h + 1) * BLOCK, :] = q_ref[tokens, lanes]
            out_ref[at, ROWS + h * BLOCK:ROWS + (h + 1) * BLOCK, :] = g
            parts.append(g.astype(F32) * o_ref[tokens, lanes].astype(F32))
        delta = jnp.sum(jnp.concatenate(parts, 0).T, axis=0, keepdims=True)
        rows = []
        rest = delta
        for _ in range(3):
            part = rest.astype(BF16).astype(F32)
            rest = rest - part
            rows += [part[:, c * DH:(c + 1) * DH] for c in range(ROWS // DH)]
        rows.append(jnp.zeros((16 - len(rows), DH), F32))
        out_ref[at, 2 * ROWS:, :] = jnp.concatenate(rows, 0).astype(BF16)


def make_messages(queries, out_grad, outputs):
    shape = jax.ShapeDtypeStruct((2 // HALVES, MESSAGE, DH), BF16)
    return pl.pallas_call(
        message_kernel,
        out_shape=(shape,) * HALVES,
        in_specs=[VMEM] * 3,
        out_specs=(VMEM,) * HALVES,
        compiler_params=params(),
        name="make_messages",
    )(queries, out_grad, outputs)


def finish_kernel(*refs):
    out_ref = refs[-1]
    for blk in range(2):
        per_half = 2 // HALVES
        half, at = blk // per_half, blk % per_half
        own, *others = refs[half * 4:half * 4 + 4]
        total = own[at]
        for other in others:
            total = total + other[at].astype(F32)
        total = total.T.astype(BF16)
        for h in range(HEADS):
            out_ref[blk * BLOCK:(blk + 1) * BLOCK, h * DH:(h + 1) * DH] = total[h * BLOCK:(h + 1) * BLOCK]


def finish_queries(parts):
    return pl.pallas_call(
        finish_kernel,
        out_shape=jax.ShapeDtypeStruct((2 * BLOCK, HEADS * DH), BF16),
        in_specs=[VMEM] * len(parts),
        out_specs=VMEM,
        compiler_params=params(),
        name="finish_queries",
    )(*parts)


def sort_blocks(rank_ref, src, lanes, dst, nk):
    def body(j, c):
        r = pl.multiple_of(rank_ref[j] * BLOCK, BLOCK)
        dst[pl.ds(r, BLOCK), :] = src[pl.ds(pl.multiple_of(j * BLOCK, BLOCK), BLOCK), lanes]
        return c

    lax.fori_loop(0, nk, body, 0, unroll=4)


def fill_work(n_ref, qp_ref, wb, wt, wq, nq):
    wb[0] = 0
    wt[0] = 0
    wq[0] = -1

    def block(b, w):
        count = (n_ref[b] + KB - 1) // KB

        def tile(t, c):
            wb[w + t] = b
            wt[w + t] = t
            wq[w + t] = qp_ref[b]
            return c

        lax.fori_loop(0, count, tile, 0)
        return w + count

    end = lax.fori_loop(0, nq, block, 1)
    for i in range(UNROLL + 1):
        wb[end + i] = 0
        wt[end + i] = 0
        wq[end + i] = -1
    return end


def run_work(end, prepare, use):
    def body(i, c):
        for u in range(UNROLL):
            w = i * UNROLL + u
            prepare(w + 1, (u + 1) % 2)
            use(w, u % 2)
        return c

    lax.fori_loop(0, (end + UNROLL - 1) // UNROLL, body, 0)


def work_scratch(nq, nk):
    size = nq * ((nk + KB - 1) // KB) + UNROLL + 2
    return [pltpu.SMEM((size,), jnp.int32)] * 3


def difference():
    key = lax.broadcasted_iota(jnp.int32, (BLOCK, ROWS), 0)
    query = lax.broadcasted_iota(jnp.int32, (BLOCK, ROWS), 1) % BLOCK
    return key - query


def causal(s, place_ref, t, query_place, diff):
    parts = []
    for u in range(KB):
        place = place_ref[t * KB + u]
        limit = jnp.where(place < query_place, BLOCK, jnp.where(place == query_place, 0, -2 * BLOCK))
        parts.append(jnp.where(diff <= limit, s[u * BLOCK:(u + 1) * BLOCK], NEG))
    return jnp.concatenate(parts, 0)


def lse_kernel(nq, nk, rank_ref, place_ref, n_ref, qp_ref, *refs):
    pieces, (kv_ref, lse_ref, q_all, ks, s_buf, diff, l8, m8, wb, wt, wq) = refs[:8], refs[8:]
    per = nq // 8
    for i, piece in enumerate(pieces):
        q_all[i * per:(i + 1) * per] = piece[:, :ROWS, :]
    sort_blocks(rank_ref, kv_ref, slice(0, DH), ks, nk)
    diff[...] = difference()
    l8[...] = jnp.zeros_like(l8)
    end = fill_work(n_ref, qp_ref, wb, wt, wq, nq)

    def prepare(w, slot):
        keys = ks[pl.ds(pl.multiple_of(wt[w] * KT, KT), KT), :]
        s_buf[slot] = nt(keys, q_all[wb[w]])

    def use(w, slot):
        s = causal(s_buf[slot] * C2, place_ref, wt[w], wq[w], diff[...])
        l8[wb[w]] += jnp.sum(jnp.exp2(s).reshape(KT // 8, 8, ROWS), axis=0)

    run_work(end, prepare, use)
    fine = jnp.ones((1, ROWS), F32)
    for b in range(nq):
        total = jnp.sum(l8[b], axis=0, keepdims=True)
        seen = n_ref[b] > 0
        inside = jnp.where((total > 1e-18) & (total < 1e30), 1.0, 0.0)
        fine = jnp.minimum(fine, jnp.where(seen, inside, 1.0))
        lse_ref[b] = jnp.where(seen, jnp.log2(total), NEG)

    @pl.when(jnp.min(fine) < 0.5)
    def _():
        def block(b, c):
            m8[...] = jnp.full_like(m8, 0.5 * NEG)
            l8[0] = jnp.zeros((8, ROWS), F32)

            def tile(t, c):
                keys = ks[pl.ds(pl.multiple_of(t * KT, KT), KT), :]
                s = causal(nt(keys, q_all[b]) * C2, place_ref, t, qp_ref[b], diff[...])
                s = s.reshape(KT // 8, 8, ROWS)
                m = m8[...]
                top = jnp.maximum(m, jnp.max(s, axis=0))
                l8[0] = l8[0] * jnp.exp2(m - top) + jnp.sum(jnp.exp2(s - top[None]), axis=0)
                m8[...] = top
                return c

            lax.fori_loop(0, (n_ref[b] + KB - 1) // KB, tile, 0)
            m = m8[...]
            top = jnp.max(m, axis=0, keepdims=True)
            total = jnp.sum(l8[0] * jnp.exp2(m - top), axis=0, keepdims=True)
            lse_ref[b] = jnp.where(n_ref[b] > 0, top + jnp.log2(total), NEG)
            return c

        lax.fori_loop(0, nq, block, 0)


def local_lse(scalars, pieces, kv):
    nq = 8 * pieces[0].shape[0]
    count = kv.shape[0]
    nk = count // BLOCK
    return pl.pallas_call(
        functools.partial(lse_kernel, nq, nk),
        out_shape=jax.ShapeDtypeStruct((nq, 1, ROWS), F32),
        in_specs=[SMEM] * 4 + [VMEM] * 9,
        out_specs=VMEM,
        scratch_shapes=[
            pltpu.VMEM((nq, ROWS, DH), BF16),
            pltpu.VMEM((count, DH), BF16),
            pltpu.VMEM((2, KT, ROWS), F32),
            pltpu.VMEM((BLOCK, ROWS), jnp.int32),
            pltpu.VMEM((nq, 8, ROWS), F32),
            pltpu.VMEM((8, ROWS), F32),
        ]
        + work_scratch(nq, nk),
        compiler_params=params(),
        cost_estimate=cost(1, nq, count),
        name="local_lse",
    )(*scalars, *pieces, kv)


def grad_kernel(nq, nk, first, last, rank_ref, place_ref, n_ref, qp_ref, *refs):
    pieces, refs = refs[:8], refs[8:]
    lse_ref, kv_ref, refs = refs[0], refs[1], refs[2:]
    if not first:
        sums_in, refs = refs[0], refs[1:]
    keep_ref, send_ref, kv_out, refs = refs[0], refs[1], refs[2], refs[3:]
    qg, delta, ks, vs, kst, sums, dqa, s_buf, dp_buf, diff, wb, wt, wq = refs
    per = nq // 8
    for i, piece in enumerate(pieces):
        for j in range(per):
            b = i * per + j
            qg[b] = piece[j, :2 * ROWS, :]
            tail = piece[j, 2 * ROWS:, :].astype(F32)
            n = ROWS // DH
            tail = tail[0:n] + tail[n:2 * n] + tail[2 * n:3 * n]
            for c in range(n):
                delta[b, :, c * DH:(c + 1) * DH] = tail[c:c + 1]
    sort_blocks(rank_ref, kv_ref, slice(0, DH), ks, nk)
    sort_blocks(rank_ref, kv_ref, slice(DH, 2 * DH), vs, nk)
    kst[...] = ks[...].T
    sums[...] = jnp.zeros_like(sums) if first else sums_in[...]
    dqa[...] = jnp.zeros_like(dqa)
    s_buf[0] = jnp.zeros((KT, ROWS), F32)
    dp_buf[0] = jnp.zeros((KT, ROWS), F32)
    diff[...] = difference()
    end = fill_work(n_ref, qp_ref, wb, wt, wq, nq)

    def prepare(w, slot):
        at = pl.ds(pl.multiple_of(wt[w] * KT, KT), KT)
        b = wb[w]
        s_buf[slot] = nt(ks[at, :], qg[b, :ROWS, :])
        dp_buf[slot] = nt(vs[at, :], qg[b, ROWS:, :])

    def use(w, slot):
        at = pl.ds(pl.multiple_of(wt[w] * KT, KT), KT)
        b = wb[w]
        p = jnp.exp2(causal(s_buf[slot] * C2 - lse_ref[b], place_ref, wt[w], wq[w], diff[...]))
        ds = (p * (dp_buf[slot] - delta[b])).astype(BF16)
        sums[1, at, :] += nn(p.astype(BF16), qg[b, ROWS:, :])
        sums[0, at, :] += nn(ds, qg[b, :ROWS, :])
        dqa[b] += nn(kst[:, at], ds)

    run_work(end, prepare, use)
    for i in range(4):
        for j in range(per):
            keep_ref[i, j] = dqa[2 * i * per + j] * SCALE
            send_ref[i, j] = dqa[(2 * i + 1) * per + j] * SCALE
    if not last:
        kv_out[...] = sums[...]
        return

    def body(j, c):
        r = pl.ds(pl.multiple_of(rank_ref[j] * BLOCK, BLOCK), BLOCK)
        at = pl.ds(pl.multiple_of(j * BLOCK, BLOCK), BLOCK)
        kv_out[at, :DH] = (sums[0, r, :] * SCALE).astype(BF16)
        kv_out[at, DH:] = sums[1, r, :].astype(BF16)
        return c

    lax.fori_loop(0, nk, body, 0, unroll=2)


def local_grads(scalars, pieces, lse, kv, sums, last):
    nq = 8 * pieces[0].shape[0]
    count = kv.shape[0]
    nk = count // BLOCK
    first = sums is None
    query_shape = jax.ShapeDtypeStruct((4, nq // 8, DH, ROWS), F32)
    if last:
        kv_shape = jax.ShapeDtypeStruct((count, 2 * DH), BF16)
    else:
        kv_shape = jax.ShapeDtypeStruct((2, count, DH), F32)
    return pl.pallas_call(
        functools.partial(grad_kernel, nq, nk, first, last),
        out_shape=(query_shape, query_shape, kv_shape),
        in_specs=[SMEM] * 4 + [VMEM] * (10 if first else 11),
        out_specs=(VMEM,) * 3,
        scratch_shapes=[
            pltpu.VMEM((nq, 2 * ROWS, DH), BF16),
            pltpu.VMEM((nq, 1, ROWS), F32),
            pltpu.VMEM((count, DH), BF16),
            pltpu.VMEM((count, DH), BF16),
            pltpu.VMEM((DH, count), BF16),
            pltpu.VMEM((2, count, DH), F32),
            pltpu.VMEM((nq, DH, ROWS), F32),
            pltpu.VMEM((2, KT, ROWS), F32),
            pltpu.VMEM((2, KT, ROWS), F32),
            pltpu.VMEM((BLOCK, ROWS), jnp.int32),
        ]
        + work_scratch(nq, nk),
        compiler_params=params(),
        cost_estimate=cost(5, nq, count),
        name="local_grads",
    )(*scalars, *pieces, lse, kv, *(() if first else (sums,)))


def along(axis, shift, size, array):
    return lax.ppermute(array, axis, [(i, (i + shift) % size) for i in range(size)])


def combine(parts):
    top = functools.reduce(jnp.maximum, parts)
    return top + jnp.log2(sum(jnp.exp2(part - top) for part in parts))


def all_lse(part):
    shape = part.shape
    part = part.reshape(4, 2, -1, ROWS)
    part = combine([part, along("core", 1, 2, part)[:, ::-1]])
    around = [part] + [jnp.roll(along("y", -d, 4, part), -d, axis=0) for d in (1, 2, 3)]
    return combine(around).reshape(shape)


def shards(queries, keys, values, outputs, out_grad, block_order):
    x, zl, core, zh, y = (lax.axis_index(a) for a in ("x", "zl", "core", "zh", "y"))

    pair = jnp.concatenate([keys, values], axis=1)
    kv = lax.all_to_all(jnp.tile(pair, (16, 1)), KEY_AXES, 0, 0, tiled=True)

    halves = []
    for message in make_messages(queries, out_grad, outputs):
        pieces = [message] + [along("y", s, 4, message) for s in (1, 3, 2)]
        pieces = [pieces[i] for i in (0, 1, 3, 2)]
        halves.append([a for piece in pieces for a in (piece, along("core", 1, 2, piece))])

    order = block_order.reshape(4, 2, 2, 2, 4, 2)
    key_place = lax.dynamic_slice(order, (0, 0, core, 0, y, 0), (4, 2, 1, 2, 1, 2)).reshape(32)
    here = lax.dynamic_slice(order, (x, zl, 0, zh, 0, 0), (1, 1, 2, 1, 4, 2)).reshape(2, 4, 2)
    here = jnp.stack([jnp.stack([here[core ^ c, (y - s) % 4] for c in range(2)]) for s in range(4)])
    rank = jnp.sum(key_place[:, None] < key_place[None, :], axis=0, dtype=jnp.int32)
    spots = lax.broadcasted_iota(jnp.int32, (32, 32), 0)
    place = jnp.sum(jnp.where(rank[None, :] == spots, key_place[None, :], 0), axis=1, dtype=jnp.int32)
    per = 2 // HALVES
    scalars = []
    for half in range(HALVES):
        query_place = here[:, :, half * per:(half + 1) * per].reshape(8 * per)
        visible = jnp.sum(key_place[None, :] <= query_place[:, None], axis=1, dtype=jnp.int32)
        scalars.append((rank, place, visible, query_place))

    sums = [all_lse(local_lse(sc, pieces, kv)) for sc, pieces in zip(scalars, halves)]

    kv_part = None
    query_parts = []
    for half in range(HALVES):
        keep, send, kv_part = local_grads(
            scalars[half], halves[half], sums[half], kv, kv_part, half == HALVES - 1
        )
        part = keep + along("core", 1, 2, send)
        query_parts += [part[0]] + [along("y", -s, 4, part[s].astype(BF16)) for s in (1, 3, 2)]
    terms = lax.all_to_all(kv_part, KEY_AXES, 0, 0, tiled=True)
    kv_grad = jnp.sum(terms.astype(F32).reshape(16, 2 * BLOCK, 2 * DH), axis=0)
    return finish_queries(query_parts), kv_grad[:, :DH], kv_grad[:, DH:]


def solution(mesh):
    fine = Mesh(mesh.devices.reshape(4, 2, 2, 2, 4), ("x", "zl", "core", "zh", "y"))
    rows = P(("x", "zl", "core", "zh", "y"), None)
    return jax.shard_map(
        shards,
        mesh=fine,
        in_specs=(rows,) * 5 + (P(),),
        out_specs=(rows,) * 3,
        check_vma=False,
    )
```

```python
import functools
import math

import jax
import jax.numpy as jnp
from jax import lax
from jax.experimental import pallas as pl
from jax.experimental.pallas import tpu as pltpu
from jax.sharding import Mesh, PartitionSpec as P

DH = 128
HEADS = 8
BLOCK = 64
ROWS = HEADS * BLOCK
GRAD_ROWS = ROWS + 16
SCALE = DH ** -0.5
C2 = SCALE * math.log2(math.e)
NEG = -1e30
KB = 4
KT = KB * BLOCK
UNROLL = 8
VMEM_LIMIT = 56 * 1024 * 1024
F32 = jnp.float32
BF16 = jnp.bfloat16
KEY_AXES = ("x", "zl", "zh")
SMEM = pl.BlockSpec(memory_space=pltpu.SMEM)
VMEM = pl.BlockSpec(memory_space=pltpu.VMEM)


def nn(a, b):
    return lax.dot_general(a, b, (((1,), (0,)), ((), ())), preferred_element_type=F32)


def nt(a, b):
    return lax.dot_general(a, b, (((1,), (1,)), ((), ())), preferred_element_type=F32)


def params():
    return pltpu.CompilerParams(vmem_limit_bytes=VMEM_LIMIT)


def cost(products, nq, count):
    area = nq * ROWS * count // 2
    return pl.CostEstimate(flops=products * 4 * area * DH, bytes_accessed=8 << 20, transcendentals=area)


def message_kernel(q_ref, g_ref, o_ref, query_ref, grad_ref):
    for blk in range(2):
        tokens = slice(blk * BLOCK, (blk + 1) * BLOCK)
        parts = []
        for h in range(HEADS):
            lanes = slice(h * DH, (h + 1) * DH)
            g = g_ref[tokens, lanes]
            query_ref[blk, h * BLOCK:(h + 1) * BLOCK, :] = q_ref[tokens, lanes]
            grad_ref[blk, h * BLOCK:(h + 1) * BLOCK, :] = g
            parts.append(g.astype(F32) * o_ref[tokens, lanes].astype(F32))
        delta = jnp.sum(jnp.concatenate(parts, 0).T, axis=0, keepdims=True)
        rows = []
        rest = delta
        for _ in range(3):
            part = rest.astype(BF16).astype(F32)
            rest = rest - part
            rows += [part[:, c * DH:(c + 1) * DH] for c in range(ROWS // DH)]
        rows.append(jnp.zeros((16 - len(rows), DH), F32))
        grad_ref[blk, ROWS:, :] = jnp.concatenate(rows, 0).astype(BF16)


def make_messages(queries, out_grad, outputs):
    return pl.pallas_call(
        message_kernel,
        out_shape=(
            jax.ShapeDtypeStruct((2, ROWS, DH), BF16),
            jax.ShapeDtypeStruct((2, GRAD_ROWS, DH), BF16),
        ),
        in_specs=[VMEM] * 3,
        out_specs=(VMEM,) * 2,
        compiler_params=params(),
        name="make_messages",
    )(queries, out_grad, outputs)


def finish_kernel(*refs):
    out_ref = refs[-1]
    for blk in range(2):
        total = refs[0][blk]
        for other in refs[1:4]:
            total = total + other[blk].astype(F32)
        total = total.T.astype(BF16)
        for h in range(HEADS):
            out_ref[blk * BLOCK:(blk + 1) * BLOCK, h * DH:(h + 1) * DH] = total[h * BLOCK:(h + 1) * BLOCK]


def finish_queries(parts):
    return pl.pallas_call(
        finish_kernel,
        out_shape=jax.ShapeDtypeStruct((2 * BLOCK, HEADS * DH), BF16),
        in_specs=[VMEM] * 4,
        out_specs=VMEM,
        compiler_params=params(),
        name="finish_queries",
    )(*parts)


def sort_blocks(table, src, lanes, dst, start, nk):
    def body(j, c):
        r = pl.multiple_of(table.rank(start + j) * BLOCK, BLOCK)
        dst[pl.ds(r, BLOCK), :] = src[pl.ds(pl.multiple_of(j * BLOCK, BLOCK), BLOCK), lanes]
        return c

    lax.fori_loop(0, nk, body, 0, unroll=4)


class Table:
    def __init__(self, ref, nq, nk):
        size = list_size(nq, nk)
        starts = [0]
        for n in (nk, nk, nq, nq, size, size, size, 1):
            starts.append(starts[-1] + n)
        self.ref, self.starts = ref, starts

    def rank(self, j):
        return self.ref[self.starts[0] + j]

    def place(self, j):
        return self.ref[self.starts[1] + j]

    def visible(self, b):
        return self.ref[self.starts[2] + b]

    def query_place(self, b):
        return self.ref[self.starts[3] + b]

    def entry(self, w):
        return tuple(self.ref[self.starts[i] + w] for i in (4, 5, 6))

    def end(self):
        return self.ref[self.starts[7]]


def list_size(nq, nk):
    return nq * ((nk + KB - 1) // KB) + UNROLL + 2


def make_table(rank, place, query_place, key_place):
    nq, nk = query_place.shape[0], key_place.shape[0]
    visible = jnp.sum(key_place[None, :] <= query_place[:, None], axis=1, dtype=jnp.int32)
    count = (visible + KB - 1) // KB
    earlier = jnp.arange(nq)[:, None] > jnp.arange(nq)[None, :]
    start = jnp.sum(jnp.where(earlier, count[None, :], 0), axis=1, dtype=jnp.int32) + 1
    w = jnp.arange(list_size(nq, nk), dtype=jnp.int32)[:, None]
    inside = (w >= start[None, :]) & (w < (start + count)[None, :])

    def pick(a):
        return jnp.sum(jnp.where(inside, a, 0), axis=1, dtype=jnp.int32)

    ids = jnp.arange(nq, dtype=jnp.int32)[None, :]
    lists = [pick(ids), pick(w - start[None, :]), pick(query_place[None, :] + 1) - 1]
    end = jnp.sum(count, dtype=jnp.int32).reshape(1) + 1
    return jnp.concatenate([rank, place, visible, query_place, *lists, end])


def run_work(end, prepare, use):
    def steps(unroll, first):
        def body(i, c):
            for u in range(unroll):
                w = first + i * unroll + u
                prepare(w + 1, (u + 1) % 2)
                use(w, u % 2)
            return c

        return body

    long = end // UNROLL
    lax.fori_loop(0, long, steps(UNROLL, 0), 0)
    rest = long * UNROLL
    lax.fori_loop(0, (end - rest + 1) // 2, steps(2, rest), 0)


def difference():
    key = lax.broadcasted_iota(jnp.int32, (BLOCK, ROWS), 0)
    query = lax.broadcasted_iota(jnp.int32, (BLOCK, ROWS), 1) % BLOCK
    return key - query


def causal(s, table, t, query_place, diff):
    parts = []
    for u in range(KB):
        place = table.place(t * KB + u)
        limit = jnp.where(place < query_place, BLOCK, jnp.where(place == query_place, 0, -2 * BLOCK))
        parts.append(jnp.where(diff <= limit, s[u * BLOCK:(u + 1) * BLOCK], NEG))
    return jnp.concatenate(parts, 0)


def combine(parts):
    top = functools.reduce(jnp.maximum, parts)
    return top + jnp.log2(sum(jnp.exp2(part - top) for part in parts))


def lse_kernel(nq, nk, table_ref, *refs):
    table = Table(table_ref, nq, nk)
    pieces, columns, refs = refs[:4], refs[4:6], refs[6:]
    lse_ref, ks, vs, kst, q_all, s_buf, diff, l8, m8 = refs
    for i, column in enumerate(columns):
        sort_blocks(table, column, slice(0, DH), ks, i * nk // 2, nk // 2)
        sort_blocks(table, column, slice(DH, 2 * DH), vs, i * nk // 2, nk // 2)
    kst[...] = ks[...].T
    for i, piece in enumerate(pieces):
        q_all[2 * i:2 * i + 2] = piece[...]
    diff[...] = difference()
    l8[...] = jnp.zeros_like(l8)

    def prepare(w, slot):
        b, t, _ = table.entry(w)
        keys = ks[pl.ds(pl.multiple_of(t * KT, KT), KT), :]
        s_buf[slot] = nt(keys, q_all[b])

    def use(w, slot):
        b, t, qp = table.entry(w)
        s = causal(s_buf[slot] * C2, table, t, qp, diff[...])
        l8[b] += jnp.sum(jnp.exp2(s).reshape(KT // 8, 8, ROWS), axis=0)

    run_work(table.end(), prepare, use)
    fine = jnp.ones((1, ROWS), F32)
    for b in range(nq):
        total = jnp.sum(l8[b], axis=0, keepdims=True)
        seen = table.visible(b) > 0
        inside = jnp.where((total > 1e-18) & (total < 1e30), 1.0, 0.0)
        fine = jnp.minimum(fine, jnp.where(seen, inside, 1.0))
        lse_ref[b:b + 1, :] = jnp.where(seen, jnp.log2(total), NEG)

    @pl.when(jnp.min(fine) < 0.5)
    def _():
        def block(b, c):
            m8[...] = jnp.full_like(m8, 0.5 * NEG)
            l8[0] = jnp.zeros((8, ROWS), F32)

            def tile(t, c):
                keys = ks[pl.ds(pl.multiple_of(t * KT, KT), KT), :]
                s = causal(nt(keys, q_all[b]) * C2, table, t, table.query_place(b), diff[...])
                s = s.reshape(KT // 8, 8, ROWS)
                m = m8[...]
                top = jnp.maximum(m, jnp.max(s, axis=0))
                l8[0] = l8[0] * jnp.exp2(m - top) + jnp.sum(jnp.exp2(s - top[None]), axis=0)
                m8[...] = top
                return c

            lax.fori_loop(0, (table.visible(b) + KB - 1) // KB, tile, 0)
            m = m8[...]
            top = jnp.max(m, axis=0, keepdims=True)
            total = jnp.sum(l8[0] * jnp.exp2(m - top), axis=0, keepdims=True)
            lse_ref[pl.ds(b, 1), :] = jnp.where(table.visible(b) > 0, top + jnp.log2(total), NEG)
            return c

        lax.fori_loop(0, nq, block, 0)


def local_lse(table, pieces, columns):
    nq = 8
    count = 2 * columns[0].shape[0]
    nk = count // BLOCK
    row_shape = jax.ShapeDtypeStruct((count, DH), BF16)
    return pl.pallas_call(
        functools.partial(lse_kernel, nq, nk),
        out_shape=(
            jax.ShapeDtypeStruct((nq, ROWS), F32),
            row_shape,
            row_shape,
            jax.ShapeDtypeStruct((DH, count), BF16),
        ),
        in_specs=[SMEM] + [VMEM] * 6,
        out_specs=(VMEM,) * 4,
        scratch_shapes=[
            pltpu.VMEM((nq, ROWS, DH), BF16),
            pltpu.VMEM((2, KT, ROWS), F32),
            pltpu.VMEM((BLOCK, ROWS), jnp.int32),
            pltpu.VMEM((nq, 8, ROWS), F32),
            pltpu.VMEM((8, ROWS), F32),
        ],
        compiler_params=params(),
        cost_estimate=cost(1, nq, count),
        name="local_lse",
    )(table, *pieces, *columns)


def grad_kernel(nq, nk, table_ref, *refs):
    table = Table(table_ref, nq, nk)
    queries, grads, refs = refs[:4], refs[4:8], refs[8:]
    sums_in, (ks, vs, kst), refs = refs[:4], refs[4:7], refs[7:]
    query_out, kv_out, kv_send, refs = refs[:4], refs[4], refs[5], refs[6:]
    q_all, g_all, lse, delta, sums, dqa, s_buf, dp_buf, diff = refs
    for i in range(4):
        for j in range(2):
            b = 2 * i + j
            lse[b] = combine([sums_in[d][b2:b2 + 1, :] for d in range(4) for b2 in [2 * ((i + d) % 4) + j]])
            q_all[b] = queries[i][j]
            g_all[b] = grads[i][j, :ROWS, :]
            tail = grads[i][j, ROWS:, :].astype(F32)
            n = ROWS // DH
            tail = tail[0:n] + tail[n:2 * n] + tail[2 * n:3 * n]
            for c in range(n):
                delta[b, :, c * DH:(c + 1) * DH] = tail[c:c + 1]
    sums[...] = jnp.zeros_like(sums)
    dqa[...] = jnp.zeros_like(dqa)
    s_buf[0] = jnp.zeros((KT, ROWS), F32)
    dp_buf[0] = jnp.zeros((KT, ROWS), F32)
    diff[...] = difference()

    def prepare(w, slot):
        b, t, _ = table.entry(w)
        at = pl.ds(pl.multiple_of(t * KT, KT), KT)
        s_buf[slot] = nt(ks[at, :], q_all[b])
        dp_buf[slot] = nt(vs[at, :], g_all[b])

    def use(w, slot):
        b, t, qp = table.entry(w)
        at = pl.ds(pl.multiple_of(t * KT, KT), KT)
        p = jnp.exp2(causal(s_buf[slot] * C2 - lse[b], table, t, qp, diff[...]))
        ds = (p * (dp_buf[slot] - delta[b])).astype(BF16)
        sums[1, at, :] += nn(p.astype(BF16), g_all[b])
        sums[0, at, :] += nn(ds, q_all[b])
        dqa[b] += nn(kst[:, at], ds)

    run_work(table.end(), prepare, use)
    for i in range(4):
        for j in range(2):
            query_out[i][j] = (dqa[2 * i + j] * SCALE).astype(query_out[i].dtype)

    for i, out in enumerate((kv_out, kv_send)):
        def body(j, c):
            r = pl.ds(pl.multiple_of(table.rank(i * nk // 2 + j) * BLOCK, BLOCK), BLOCK)
            at = pl.ds(pl.multiple_of(j * BLOCK, BLOCK), BLOCK)
            out[at, :DH] = (sums[0, r, :] * SCALE).astype(out.dtype)
            out[at, DH:] = sums[1, r, :].astype(out.dtype)
            return c

        lax.fori_loop(0, nk // 2, body, 0, unroll=2)


def local_grads(table, queries, grads, sums, sorted_keys):
    nq = 8
    count = sorted_keys[0].shape[0]
    nk = count // BLOCK
    return pl.pallas_call(
        functools.partial(grad_kernel, nq, nk),
        out_shape=tuple(jax.ShapeDtypeStruct((2, DH, ROWS), F32 if i == 0 else BF16) for i in range(4))
        + tuple(jax.ShapeDtypeStruct((count // 2, 2 * DH), t) for t in (F32, BF16)),
        in_specs=[SMEM] + [VMEM] * 15,
        out_specs=(VMEM,) * 6,
        scratch_shapes=[
            pltpu.VMEM((nq, ROWS, DH), BF16),
            pltpu.VMEM((nq, ROWS, DH), BF16),
            pltpu.VMEM((nq, 1, ROWS), F32),
            pltpu.VMEM((nq, 1, ROWS), F32),
            pltpu.VMEM((2, count, DH), F32),
            pltpu.VMEM((nq, DH, ROWS), F32),
            pltpu.VMEM((2, KT, ROWS), F32),
            pltpu.VMEM((2, KT, ROWS), F32),
            pltpu.VMEM((BLOCK, ROWS), jnp.int32),
        ],
        compiler_params=params(),
        cost_estimate=cost(5, nq, count),
        name="local_grads",
    )(table, *queries, *grads, *sums, *sorted_keys)


def along(axis, shift, size, array):
    return lax.ppermute(array, axis, [(i, (i + shift) % size) for i in range(size)])


def gather_y(own):
    one, three, two = (along("y", s, 4, own) for s in (1, 3, 2))
    return [own, one, two, three]


def shards(queries, keys, values, outputs, out_grad, block_order):
    x, zl, core, zh, y = (lax.axis_index(a) for a in ("x", "zl", "core", "zh", "y"))
    fence = lax.optimization_barrier

    pair = jnp.concatenate([keys, values], axis=1)
    column = lax.all_to_all(jnp.tile(pair, (16, 1)), KEY_AXES, 0, 0, tiled=True)
    columns = [column, along("core", 1, 2, column)]

    order = block_order.reshape(4, 2, 2, 2, 4, 2)
    key_place = lax.dynamic_slice(order, (0, 0, 0, 0, y, 0), (4, 2, 2, 2, 1, 2))
    key_place = jnp.moveaxis(key_place, 2, 0).reshape(2, 32)
    key_place = jnp.where(core == 0, key_place, key_place[::-1]).reshape(64)
    here = lax.dynamic_slice(order, (x, zl, core, zh, 0, 0), (1, 1, 1, 1, 4, 2)).reshape(4, 2)
    query_place = jnp.stack([here[(y - s) % 4] for s in range(4)]).reshape(8)
    rank = jnp.sum(key_place[:, None] < key_place[None, :], axis=0, dtype=jnp.int32)
    spots = lax.broadcasted_iota(jnp.int32, (64, 64), 0)
    place = jnp.sum(jnp.where(rank[None, :] == spots, key_place[None, :], 0), axis=1, dtype=jnp.int32)
    table = make_table(rank, place, query_place, key_place)

    query_message, grad_message = make_messages(queries, out_grad, outputs)
    query_pieces = gather_y(query_message)
    grad_pieces = gather_y(grad_message)

    (part, *sorted_keys), grad_pieces[1:] = fence((local_lse(table, query_pieces, columns), grad_pieces[1:]))
    sums = [part] + [along("y", -d, 4, part) for d in (1, 2, 3)]

    *query_parts, kv_part, kv_send = local_grads(table, query_pieces, grad_pieces, sums, sorted_keys)
    query_parts = [query_parts[0]] + [along("y", -s, 4, query_parts[s]) for s in (1, 3, 2)]
    kv_part = (kv_part + along("core", 1, 2, kv_send).astype(F32)).astype(BF16)
    terms = lax.all_to_all(kv_part, KEY_AXES, 0, 0, tiled=True)
    kv_grad = jnp.sum(terms.astype(F32).reshape(16, 2 * BLOCK, 2 * DH), axis=0)
    return finish_queries(query_parts), kv_grad[:, :DH], kv_grad[:, DH:]


def solution(mesh):
    fine = Mesh(mesh.devices.reshape(4, 2, 2, 2, 4), ("x", "zl", "core", "zh", "y"))
    rows = P(("x", "zl", "core", "zh", "y"), None)
    return jax.shard_map(
        shards,
        mesh=fine,
        in_specs=(rows,) * 5 + (P(),),
        out_specs=(rows,) * 3,
        check_vma=False,
    )
```

```python
import functools
import math

import jax
import jax.numpy as jnp
from jax import lax
from jax.experimental import pallas as pl
from jax.experimental.pallas import tpu as pltpu
from jax.sharding import Mesh, PartitionSpec as P

DH = 128
HEADS = 8
BLOCK = 64
ROWS = HEADS * BLOCK
GRAD_ROWS = ROWS + 16
DEPTH = 3
SCALE = DH ** -0.5
C2 = SCALE * math.log2(math.e)
NEG = -1e30
KB = 4
KT = KB * BLOCK
UNROLL = 8
VMEM_LIMIT = 56 * 1024 * 1024
F32 = jnp.float32
BF16 = jnp.bfloat16
KEY_AXES = ("x", "zl", "zh")
ANY = pl.BlockSpec(memory_space=pl.ANY)
SMEM = pl.BlockSpec(memory_space=pltpu.SMEM)
VMEM = pl.BlockSpec(memory_space=pltpu.VMEM)


def nn(a, b):
    return lax.dot_general(a, b, (((1,), (0,)), ((), ())), preferred_element_type=F32)


def nt(a, b):
    return lax.dot_general(a, b, (((1,), (1,)), ((), ())), preferred_element_type=F32)


def params():
    return pltpu.CompilerParams(vmem_limit_bytes=VMEM_LIMIT)


def cost(products, nq, count):
    area = nq * ROWS * count // 2
    return pl.CostEstimate(flops=products * 4 * area * DH, bytes_accessed=8 << 20, transcendentals=area)


def message_kernel(q_ref, g_ref, o_ref, query_ref, grad_ref):
    for blk in range(2):
        tokens = slice(blk * BLOCK, (blk + 1) * BLOCK)
        parts = []
        for h in range(HEADS):
            lanes = slice(h * DH, (h + 1) * DH)
            g = g_ref[tokens, lanes]
            query_ref[blk, h * BLOCK:(h + 1) * BLOCK, :] = q_ref[tokens, lanes]
            grad_ref[blk, h * BLOCK:(h + 1) * BLOCK, :] = g
            parts.append(g.astype(F32) * o_ref[tokens, lanes].astype(F32))
        delta = jnp.sum(jnp.concatenate(parts, 0).T, axis=0, keepdims=True)
        rows = []
        rest = delta
        for _ in range(3):
            part = rest.astype(BF16).astype(F32)
            rest = rest - part
            rows += [part[:, c * DH:(c + 1) * DH] for c in range(ROWS // DH)]
        rows.append(jnp.zeros((16 - len(rows), DH), F32))
        grad_ref[blk, ROWS:, :] = jnp.concatenate(rows, 0).astype(BF16)


def make_messages(queries, out_grad, outputs):
    return pl.pallas_call(
        message_kernel,
        out_shape=(
            jax.ShapeDtypeStruct((2, ROWS, DH), BF16),
            jax.ShapeDtypeStruct((2, GRAD_ROWS, DH), BF16),
        ),
        in_specs=[VMEM] * 3,
        out_specs=(VMEM,) * 2,
        compiler_params=params(),
        name="make_messages",
    )(queries, out_grad, outputs)


def finish_kernel(*refs):
    out_ref = refs[-1]
    for blk in range(2):
        total = refs[0][blk]
        for other in refs[1:4]:
            total = total + other[blk].astype(F32)
        total = total.T.astype(BF16)
        for h in range(HEADS):
            out_ref[blk * BLOCK:(blk + 1) * BLOCK, h * DH:(h + 1) * DH] = total[h * BLOCK:(h + 1) * BLOCK]


def finish_queries(parts):
    return pl.pallas_call(
        finish_kernel,
        out_shape=jax.ShapeDtypeStruct((2 * BLOCK, HEADS * DH), BF16),
        in_specs=[VMEM] * 4,
        out_specs=VMEM,
        compiler_params=params(),
        name="finish_queries",
    )(*parts)


def sort_blocks(table, src, lanes, dst, start, nk):
    def body(j, c):
        r = pl.multiple_of(table.rank(start + j) * BLOCK, BLOCK)
        dst[pl.ds(r, BLOCK), :] = src[pl.ds(pl.multiple_of(j * BLOCK, BLOCK), BLOCK), lanes]
        return c

    lax.fori_loop(0, nk, body, 0, unroll=4)


class Table:
    def __init__(self, ref, nq, nk):
        size = list_size(nq, nk)
        starts = [0]
        for n in (nk, nk, nq, nq, size, size, size, 1):
            starts.append(starts[-1] + n)
        self.ref, self.starts = ref, starts

    def rank(self, j):
        return self.ref[self.starts[0] + j]

    def place(self, j):
        return self.ref[self.starts[1] + j]

    def visible(self, b):
        return self.ref[self.starts[2] + b]

    def query_place(self, b):
        return self.ref[self.starts[3] + b]

    def entry(self, w):
        return tuple(self.ref[self.starts[i] + w] for i in (4, 5, 6))

    def end(self):
        return self.ref[self.starts[7]]


def list_size(nq, nk):
    most = nq * ((nk + KB - 1) // KB) + 1
    return (most + UNROLL - 1) // UNROLL * UNROLL + 1


def group_count(nq, nk):
    return list_size(nq, nk) // UNROLL


def make_table(rank, place, query_place, key_place):
    nq, nk = query_place.shape[0], key_place.shape[0]
    visible = jnp.sum(key_place[None, :] <= query_place[:, None], axis=1, dtype=jnp.int32)
    count = (visible + KB - 1) // KB
    earlier = jnp.arange(nq)[:, None] > jnp.arange(nq)[None, :]
    start = jnp.sum(jnp.where(earlier, count[None, :], 0), axis=1, dtype=jnp.int32) + 1
    w = jnp.arange(list_size(nq, nk), dtype=jnp.int32)[:, None]
    inside = (w >= start[None, :]) & (w < (start + count)[None, :])

    def pick(a):
        return jnp.sum(jnp.where(inside, a, 0), axis=1, dtype=jnp.int32)

    ids = jnp.arange(nq, dtype=jnp.int32)[None, :]
    lists = [pick(ids), pick(w - start[None, :]), pick(query_place[None, :] + 1) - 1]
    end = jnp.sum(count, dtype=jnp.int32).reshape(1) + 1
    return jnp.concatenate([rank, place, visible, query_place, *lists, end])


def run_work(end, prepare, use, before, after):
    def body(i, c):
        slot = lax.rem(i, DEPTH)
        before(i, slot)
        for u in range(UNROLL):
            prepare(i * UNROLL + u + 1, (u + 1) % 2)
            use(i * UNROLL + u, u % 2, (slot, u))
        after(i, slot)
        return c

    whole = end // UNROLL
    lax.fori_loop(0, whole, body, 0)
    rest = end - whole * UNROLL

    @pl.when(rest > 0)
    def _():
        slot = lax.rem(whole, DEPTH)
        before(whole, slot)

        def pair(i, c):
            for u in range(2):
                w = whole * UNROLL + 2 * i + u
                prepare(w + 1, (u + 1) % 2)
                use(w, u % 2, (slot, 2 * i + u))
            return c

        lax.fori_loop(0, (rest + 1) // 2, pair, 0)
        after(whole, slot)


def bodies(end):
    return (end + UNROLL - 1) // UNROLL


def difference():
    key = lax.broadcasted_iota(jnp.int32, (BLOCK, ROWS), 0)
    query = lax.broadcasted_iota(jnp.int32, (BLOCK, ROWS), 1) % BLOCK
    return key - query


def causal(s, table, t, query_place, diff):
    parts = []
    for u in range(KB):
        place = table.place(t * KB + u)
        limit = jnp.where(place < query_place, BLOCK, jnp.where(place == query_place, 0, -2 * BLOCK))
        parts.append(jnp.where(diff <= limit, s[u * BLOCK:(u + 1) * BLOCK], NEG))
    return jnp.concatenate(parts, 0)


def combine(parts):
    top = functools.reduce(jnp.maximum, parts)
    return top + jnp.log2(sum(jnp.exp2(part - top) for part in parts))


def lse_kernel(nq, nk, table_ref, *refs):
    table = Table(table_ref, nq, nk)
    pieces, columns, refs = refs[:4], refs[4:6], refs[6:]
    lse_ref, shift_ref, e_ref, ks, vs, kst, q_all, s_buf, diff, l8, m8, e_buf, e_sem = refs
    for i, column in enumerate(columns):
        sort_blocks(table, column, slice(0, DH), ks, i * nk // 2, nk // 2)
        sort_blocks(table, column, slice(DH, 2 * DH), vs, i * nk // 2, nk // 2)
    kst[...] = ks[...].T
    for i, piece in enumerate(pieces):
        q_all[2 * i:2 * i + 2] = piece[...]
    diff[...] = difference()
    l8[...] = jnp.zeros_like(l8)

    def send(i, slot):
        return pltpu.make_async_copy(e_buf.at[slot], e_ref.at[i], e_sem.at[slot])

    def free(i, slot):
        @pl.when(i >= DEPTH)
        def _():
            send(i, slot).wait()

    def prepare(w, slot):
        b, t, _ = table.entry(w)
        keys = ks[pl.ds(pl.multiple_of(t * KT, KT), KT), :]
        s_buf[slot] = nt(keys, q_all[b])

    def use(w, slot, ring):
        b, t, qp = table.entry(w)
        e = jnp.exp2(causal(s_buf[slot] * C2, table, t, qp, diff[...]))
        l8[b] += jnp.sum(e.reshape(KT // 8, 8, ROWS), axis=0)
        e_buf[ring] = e.astype(BF16)

    run_work(
        table.end(), prepare, use, free, lambda i, slot: send(i, slot).start()
    )
    for slot in range(DEPTH):

        @pl.when(slot < bodies(table.end()))
        def _():
            send(slot, slot).wait()

    shift_ref[...] = jnp.zeros_like(shift_ref)
    fine = jnp.ones((1, ROWS), F32)
    for b in range(nq):
        total = jnp.sum(l8[b], axis=0, keepdims=True)
        seen = table.visible(b) > 0
        inside = jnp.where((total > 1e-18) & (total < 1e30), 1.0, 0.0)
        fine = jnp.minimum(fine, jnp.where(seen, inside, 1.0))
        lse_ref[b:b + 1, :] = jnp.where(seen, jnp.log2(total), NEG)

    @pl.when(jnp.min(fine) < 0.5)
    def _():
        def block(b, c):
            m8[...] = jnp.full_like(m8, 0.5 * NEG)
            l8[0] = jnp.zeros((8, ROWS), F32)

            def tile(t, c):
                keys = ks[pl.ds(pl.multiple_of(t * KT, KT), KT), :]
                s = causal(nt(keys, q_all[b]) * C2, table, t, table.query_place(b), diff[...])
                s = s.reshape(KT // 8, 8, ROWS)
                m = m8[...]
                top = jnp.maximum(m, jnp.max(s, axis=0))
                l8[0] = l8[0] * jnp.exp2(m - top) + jnp.sum(jnp.exp2(s - top[None]), axis=0)
                m8[...] = top
                return c

            lax.fori_loop(0, (table.visible(b) + KB - 1) // KB, tile, 0)
            m = m8[...]
            top = jnp.max(m, axis=0, keepdims=True)
            total = jnp.sum(l8[0] * jnp.exp2(m - top), axis=0, keepdims=True)
            lse = jnp.where(table.visible(b) > 0, top + jnp.log2(total), NEG)
            lse_ref[pl.ds(b, 1), :] = lse
            shift_ref[pl.ds(b, 1), :] = lse
            return c

        lax.fori_loop(0, nq, block, 0)

        def entry(w, c):
            b, t, qp = table.entry(w)
            keys = ks[pl.ds(pl.multiple_of(t * KT, KT), KT), :]
            s = nt(keys, q_all[b]) * C2 - lse_ref[pl.ds(b, 1), :]
            e_buf[0, 0] = jnp.exp2(causal(s, table, t, qp, diff[...])).astype(BF16)
            place = e_ref.at[w // UNROLL, lax.rem(w, UNROLL)]
            copy = pltpu.make_async_copy(e_buf.at[0, 0], place, e_sem.at[0])
            copy.start()
            copy.wait()
            return c

        lax.fori_loop(1, table.end(), entry, 0)


def local_lse(table, pieces, columns):
    nq = 8
    count = 2 * columns[0].shape[0]
    nk = count // BLOCK
    row_shape = jax.ShapeDtypeStruct((count, DH), BF16)
    return pl.pallas_call(
        functools.partial(lse_kernel, nq, nk),
        out_shape=(
            jax.ShapeDtypeStruct((nq, ROWS), F32),
            jax.ShapeDtypeStruct((nq, ROWS), F32),
            jax.ShapeDtypeStruct((group_count(nq, nk), UNROLL, KT, ROWS), BF16),
            row_shape,
            row_shape,
            jax.ShapeDtypeStruct((DH, count), BF16),
        ),
        in_specs=[SMEM] + [VMEM] * 6,
        out_specs=(VMEM, VMEM, ANY) + (VMEM,) * 3,
        scratch_shapes=[
            pltpu.VMEM((nq, ROWS, DH), BF16),
            pltpu.VMEM((2, KT, ROWS), F32),
            pltpu.VMEM((BLOCK, ROWS), jnp.int32),
            pltpu.VMEM((nq, 8, ROWS), F32),
            pltpu.VMEM((8, ROWS), F32),
            pltpu.VMEM((DEPTH, UNROLL, KT, ROWS), BF16),
            pltpu.SemaphoreType.DMA((DEPTH,)),
        ],
        compiler_params=params(),
        cost_estimate=cost(1, nq, count),
        name="local_lse",
    )(table, *pieces, *columns)


def grad_kernel(nq, nk, table_ref, *refs):
    table = Table(table_ref, nq, nk)
    queries, grads, refs = refs[:4], refs[4:8], refs[8:]
    sums_in, (shift_ref, e_ref, ks, vs, kst), refs = refs[:4], refs[4:9], refs[9:]
    query_out, kv_out, kv_send, refs = refs[:4], refs[4], refs[5], refs[6:]
    q_all, g_all, factor, delta, sums, dqa, dp_buf, e_buf, e_sem = refs

    def fetch(i, slot):
        return pltpu.make_async_copy(e_ref.at[i], e_buf.at[slot], e_sem.at[slot])

    def fetch_body(i, slot):
        @pl.when(i < bodies(table.end()))
        def _():
            fetch(i, slot).start()

    for slot in range(DEPTH):
        fetch_body(slot, slot)
    for i in range(4):
        for j in range(2):
            b = 2 * i + j
            lse = combine([sums_in[d][b2:b2 + 1, :] for d in range(4) for b2 in [2 * ((i + d) % 4) + j]])
            factor[b] = jnp.exp2(shift_ref[b:b + 1, :] - lse)
            q_all[b] = queries[i][j]
            g_all[b] = grads[i][j, :ROWS, :]
            tail = grads[i][j, ROWS:, :].astype(F32)
            n = ROWS // DH
            tail = tail[0:n] + tail[n:2 * n] + tail[2 * n:3 * n]
            for c in range(n):
                delta[b, :, c * DH:(c + 1) * DH] = tail[c:c + 1]
    sums[...] = jnp.zeros_like(sums)
    dqa[...] = jnp.zeros_like(dqa)
    dp_buf[0] = jnp.zeros((KT, ROWS), F32)

    def prepare(w, slot):
        b, t, _ = table.entry(w)
        at = pl.ds(pl.multiple_of(t * KT, KT), KT)
        dp_buf[slot] = nt(vs[at, :], g_all[b])

    def use(w, slot, ring):
        b, t, _ = table.entry(w)
        at = pl.ds(pl.multiple_of(t * KT, KT), KT)
        p = e_buf[ring].astype(F32) * factor[b]
        ds = (p * (dp_buf[slot] - delta[b])).astype(BF16)
        sums[1, at, :] += nn(p.astype(BF16), g_all[b])
        sums[0, at, :] += nn(ds, q_all[b])
        dqa[b] += nn(kst[:, at], ds)

    run_work(
        table.end(),
        prepare,
        use,
        lambda i, slot: fetch(i, slot).wait(),
        lambda i, slot: fetch_body(i + DEPTH, slot),
    )
    for i in range(4):
        for j in range(2):
            query_out[i][j] = (dqa[2 * i + j] * SCALE).astype(query_out[i].dtype)

    for i, out in enumerate((kv_out, kv_send)):
        def body(j, c):
            r = pl.ds(pl.multiple_of(table.rank(i * nk // 2 + j) * BLOCK, BLOCK), BLOCK)
            at = pl.ds(pl.multiple_of(j * BLOCK, BLOCK), BLOCK)
            out[at, :DH] = (sums[0, r, :] * SCALE).astype(out.dtype)
            out[at, DH:] = sums[1, r, :].astype(out.dtype)
            return c

        lax.fori_loop(0, nk // 2, body, 0, unroll=2)


def local_grads(table, queries, grads, sums, results):
    nq = 8
    count = results[2].shape[0]
    nk = count // BLOCK
    return pl.pallas_call(
        functools.partial(grad_kernel, nq, nk),
        out_shape=tuple(jax.ShapeDtypeStruct((2, DH, ROWS), F32 if i == 0 else BF16) for i in range(4))
        + tuple(jax.ShapeDtypeStruct((count // 2, 2 * DH), t) for t in (F32, BF16)),
        in_specs=[SMEM] + [VMEM] * 13 + [ANY] + [VMEM] * 3,
        out_specs=(VMEM,) * 6,
        scratch_shapes=[
            pltpu.VMEM((nq, ROWS, DH), BF16),
            pltpu.VMEM((nq, ROWS, DH), BF16),
            pltpu.VMEM((nq, 1, ROWS), F32),
            pltpu.VMEM((nq, 1, ROWS), F32),
            pltpu.VMEM((2, count, DH), F32),
            pltpu.VMEM((nq, DH, ROWS), F32),
            pltpu.VMEM((2, KT, ROWS), F32),
            pltpu.VMEM((DEPTH, UNROLL, KT, ROWS), BF16),
            pltpu.SemaphoreType.DMA((DEPTH,)),
        ],
        compiler_params=params(),
        cost_estimate=cost(5, nq, count),
        name="local_grads",
    )(table, *queries, *grads, *sums, *results)


def along(axis, shift, size, array):
    return lax.ppermute(array, axis, [(i, (i + shift) % size) for i in range(size)])


def gather_y(own):
    one, three, two = (along("y", s, 4, own) for s in (1, 3, 2))
    return [own, one, two, three]


def shards(queries, keys, values, outputs, out_grad, block_order):
    x, zl, core, zh, y = (lax.axis_index(a) for a in ("x", "zl", "core", "zh", "y"))
    fence = lax.optimization_barrier

    pair = jnp.concatenate([keys, values], axis=1)
    column = lax.all_to_all(jnp.tile(pair, (16, 1)), KEY_AXES, 0, 0, tiled=True)
    columns = [column, along("core", 1, 2, column)]

    order = block_order.reshape(4, 2, 2, 2, 4, 2)
    key_place = lax.dynamic_slice(order, (0, 0, 0, 0, y, 0), (4, 2, 2, 2, 1, 2))
    key_place = jnp.moveaxis(key_place, 2, 0).reshape(2, 32)
    key_place = jnp.where(core == 0, key_place, key_place[::-1]).reshape(64)
    here = lax.dynamic_slice(order, (x, zl, core, zh, 0, 0), (1, 1, 1, 1, 4, 2)).reshape(4, 2)
    query_place = jnp.stack([here[(y - s) % 4] for s in range(4)]).reshape(8)
    rank = jnp.sum(key_place[:, None] < key_place[None, :], axis=0, dtype=jnp.int32)
    spots = lax.broadcasted_iota(jnp.int32, (64, 64), 0)
    place = jnp.sum(jnp.where(rank[None, :] == spots, key_place[None, :], 0), axis=1, dtype=jnp.int32)
    table = make_table(rank, place, query_place, key_place)

    query_message, grad_message = make_messages(queries, out_grad, outputs)
    query_pieces = gather_y(query_message)
    grad_pieces = gather_y(grad_message)

    (part, *results), grad_pieces[1:] = fence((local_lse(table, query_pieces, columns), grad_pieces[1:]))
    sums = [part] + [along("y", -d, 4, part) for d in (1, 2, 3)]

    *query_parts, kv_part, kv_send = local_grads(table, query_pieces, grad_pieces, sums, results)
    query_parts = [query_parts[0]] + [along("y", -s, 4, query_parts[s]) for s in (1, 3, 2)]
    kv_part = (kv_part + along("core", 1, 2, kv_send).astype(F32)).astype(BF16)
    terms = lax.all_to_all(kv_part, KEY_AXES, 0, 0, tiled=True)
    kv_grad = jnp.sum(terms.astype(F32).reshape(16, 2 * BLOCK, 2 * DH), axis=0)
    return finish_queries(query_parts), kv_grad[:, :DH], kv_grad[:, DH:]


def solution(mesh):
    fine = Mesh(mesh.devices.reshape(4, 2, 2, 2, 4), ("x", "zl", "core", "zh", "y"))
    rows = P(("x", "zl", "core", "zh", "y"), None)
    return jax.shard_map(
        shards,
        mesh=fine,
        in_specs=(rows,) * 5 + (P(),),
        out_specs=(rows,) * 3,
        check_vma=False,
    )
```

```python
import functools
import math

import jax
import jax.numpy as jnp
from jax import lax
from jax.experimental import pallas as pl
from jax.experimental.pallas import tpu as pltpu
from jax.sharding import Mesh, PartitionSpec as P

DH = 128
HEADS = 8
BLOCK = 64
ROWS = HEADS * BLOCK
GRAD_ROWS = ROWS + 16
DEPTH = 3
SCALE = DH ** -0.5
C2 = SCALE * math.log2(math.e)
NEG = -1e30
KB = 4
KT = KB * BLOCK
UNROLL = 8
VMEM_LIMIT = 56 * 1024 * 1024
F32 = jnp.float32
BF16 = jnp.bfloat16
KEY_AXES = ("x", "zl", "zh")
ANY = pl.BlockSpec(memory_space=pl.ANY)
SMEM = pl.BlockSpec(memory_space=pltpu.SMEM)
VMEM = pl.BlockSpec(memory_space=pltpu.VMEM)


def nn(a, b):
    return lax.dot_general(a, b, (((1,), (0,)), ((), ())), preferred_element_type=F32)


def nt(a, b):
    return lax.dot_general(a, b, (((1,), (1,)), ((), ())), preferred_element_type=F32)


def params():
    return pltpu.CompilerParams(vmem_limit_bytes=VMEM_LIMIT)


def cost(products, nq, count):
    area = nq * ROWS * count // 2
    return pl.CostEstimate(flops=products * 4 * area * DH, bytes_accessed=8 << 20, transcendentals=area)


def message_kernel(q_ref, g_ref, o_ref, query_ref, grad_ref):
    for blk in range(2):
        tokens = slice(blk * BLOCK, (blk + 1) * BLOCK)
        parts = []
        for h in range(HEADS):
            lanes = slice(h * DH, (h + 1) * DH)
            g = g_ref[tokens, lanes]
            query_ref[blk, h * BLOCK:(h + 1) * BLOCK, :] = q_ref[tokens, lanes]
            grad_ref[blk, h * BLOCK:(h + 1) * BLOCK, :] = g
            parts.append(g.astype(F32) * o_ref[tokens, lanes].astype(F32))
        delta = jnp.sum(jnp.concatenate(parts, 0).T, axis=0, keepdims=True)
        rows = []
        rest = delta
        for _ in range(3):
            part = rest.astype(BF16).astype(F32)
            rest = rest - part
            rows += [part[:, c * DH:(c + 1) * DH] for c in range(ROWS // DH)]
        rows.append(jnp.zeros((16 - len(rows), DH), F32))
        grad_ref[blk, ROWS:, :] = jnp.concatenate(rows, 0).astype(BF16)


def make_messages(queries, out_grad, outputs):
    return pl.pallas_call(
        message_kernel,
        out_shape=(
            jax.ShapeDtypeStruct((2, ROWS, DH), BF16),
            jax.ShapeDtypeStruct((2, GRAD_ROWS, DH), BF16),
        ),
        in_specs=[VMEM] * 3,
        out_specs=(VMEM,) * 2,
        compiler_params=params(),
        name="make_messages",
    )(queries, out_grad, outputs)


def finish_kernel(*refs):
    out_ref = refs[-1]
    for blk in range(2):
        total = refs[0][blk]
        for other in refs[1:3]:
            total = total + other[blk].astype(F32)
        total = total.T.astype(BF16)
        for h in range(HEADS):
            out_ref[blk * BLOCK:(blk + 1) * BLOCK, h * DH:(h + 1) * DH] = total[h * BLOCK:(h + 1) * BLOCK]


def finish_queries(parts):
    return pl.pallas_call(
        finish_kernel,
        out_shape=jax.ShapeDtypeStruct((2 * BLOCK, HEADS * DH), BF16),
        in_specs=[VMEM] * 3,
        out_specs=VMEM,
        compiler_params=params(),
        name="finish_queries",
    )(*parts)


def sort_blocks(table, src, lanes, dst, start, nk):
    def body(j, c):
        r = pl.multiple_of(table.rank(start + j) * BLOCK, BLOCK)
        dst[pl.ds(r, BLOCK), :] = src[pl.ds(pl.multiple_of(j * BLOCK, BLOCK), BLOCK), lanes]
        return c

    lax.fori_loop(0, nk, body, 0, unroll=4)


class Table:
    def __init__(self, ref, nq, nk):
        size = list_size(nq, nk)
        starts = [0]
        for n in (nk, nk, nq, nq, size, size, size, 1):
            starts.append(starts[-1] + n)
        self.ref, self.starts = ref, starts

    def rank(self, j):
        return self.ref[self.starts[0] + j]

    def place(self, j):
        return self.ref[self.starts[1] + j]

    def visible(self, b):
        return self.ref[self.starts[2] + b]

    def query_place(self, b):
        return self.ref[self.starts[3] + b]

    def entry(self, w):
        return tuple(self.ref[self.starts[i] + w] for i in (4, 5, 6))

    def end(self):
        return self.ref[self.starts[7]]


def list_size(nq, nk):
    most = nq * ((nk + KB - 1) // KB) + 1
    return (most + UNROLL - 1) // UNROLL * UNROLL + 1


def group_count(nq, nk):
    return list_size(nq, nk) // UNROLL


def make_table(rank, place, query_place, key_place):
    nq, nk = query_place.shape[0], key_place.shape[0]
    visible = jnp.sum(key_place[None, :] <= query_place[:, None], axis=1, dtype=jnp.int32)
    count = (visible + KB - 1) // KB
    earlier = jnp.arange(nq)[:, None] > jnp.arange(nq)[None, :]
    start = jnp.sum(jnp.where(earlier, count[None, :], 0), axis=1, dtype=jnp.int32) + 1
    w = jnp.arange(list_size(nq, nk), dtype=jnp.int32)[:, None]
    inside = (w >= start[None, :]) & (w < (start + count)[None, :])

    def pick(a):
        return jnp.sum(jnp.where(inside, a, 0), axis=1, dtype=jnp.int32)

    ids = jnp.arange(nq, dtype=jnp.int32)[None, :]
    lists = [pick(ids), pick(w - start[None, :]), pick(query_place[None, :] + 1) - 1]
    end = jnp.sum(count, dtype=jnp.int32).reshape(1) + 1
    return jnp.concatenate([rank, place, visible, query_place, *lists, end])


def run_work(end, prepare, use, before, after):
    def body(i, c):
        slot = lax.rem(i, DEPTH)
        before(i, slot)
        for u in range(UNROLL):
            prepare(i * UNROLL + u + 1, (u + 1) % 2)
            use(i * UNROLL + u, u % 2, (slot, u))
        after(i, slot)
        return c

    whole = end // UNROLL
    lax.fori_loop(0, whole, body, 0)
    rest = end - whole * UNROLL

    @pl.when(rest > 0)
    def _():
        slot = lax.rem(whole, DEPTH)
        before(whole, slot)

        def pair(i, c):
            for u in range(2):
                w = whole * UNROLL + 2 * i + u
                prepare(w + 1, (u + 1) % 2)
                use(w, u % 2, (slot, 2 * i + u))
            return c

        lax.fori_loop(0, (rest + 1) // 2, pair, 0)
        after(whole, slot)


def bodies(end):
    return (end + UNROLL - 1) // UNROLL


def difference():
    key = lax.broadcasted_iota(jnp.int32, (BLOCK, ROWS), 0)
    query = lax.broadcasted_iota(jnp.int32, (BLOCK, ROWS), 1) % BLOCK
    return key - query


def causal(s, table, t, query_place, diff):
    parts = []
    for u in range(KB):
        place = table.place(t * KB + u)
        limit = jnp.where(place < query_place, BLOCK, jnp.where(place == query_place, 0, -2 * BLOCK))
        parts.append(jnp.where(diff <= limit, s[u * BLOCK:(u + 1) * BLOCK], NEG))
    return jnp.concatenate(parts, 0)


def combine(parts):
    top = functools.reduce(jnp.maximum, parts)
    return top + jnp.log2(sum(jnp.exp2(part - top) for part in parts))


def lse_kernel(nq, nk, table_ref, *refs):
    table = Table(table_ref, nq, nk)
    pieces, columns, refs = refs[:4], refs[4:6], refs[6:]
    lse_ref, shift_ref, e_ref, ks, vs, kst, q_all, s_buf, diff, l8, m8, e_buf, e_sem = refs
    for i, column in enumerate(columns):
        sort_blocks(table, column, slice(0, DH), ks, i * nk // 2, nk // 2)
        sort_blocks(table, column, slice(DH, 2 * DH), vs, i * nk // 2, nk // 2)
    kst[...] = ks[...].T
    for i, piece in enumerate(pieces):
        q_all[2 * i:2 * i + 2] = piece[...]
    diff[...] = difference()
    l8[...] = jnp.zeros_like(l8)

    def send(i, slot):
        return pltpu.make_async_copy(e_buf.at[slot], e_ref.at[i], e_sem.at[slot])

    def free(i, slot):
        @pl.when(i >= DEPTH)
        def _():
            send(i, slot).wait()

    def prepare(w, slot):
        b, t, _ = table.entry(w)
        keys = ks[pl.ds(pl.multiple_of(t * KT, KT), KT), :]
        s_buf[slot] = nt(keys, q_all[b])

    def use(w, slot, ring):
        b, t, qp = table.entry(w)
        e = jnp.exp2(causal(s_buf[slot] * C2, table, t, qp, diff[...]))
        l8[b] += jnp.sum(e.reshape(KT // 8, 8, ROWS), axis=0)
        e_buf[ring] = e.astype(BF16)

    run_work(
        table.end(), prepare, use, free, lambda i, slot: send(i, slot).start()
    )
    for slot in range(DEPTH):

        @pl.when(slot < bodies(table.end()))
        def _():
            send(slot, slot).wait()

    shift_ref[...] = jnp.zeros_like(shift_ref)
    fine = jnp.ones((1, ROWS), F32)
    for b in range(nq):
        total = jnp.sum(l8[b], axis=0, keepdims=True)
        seen = table.visible(b) > 0
        inside = jnp.where((total > 1e-18) & (total < 1e30), 1.0, 0.0)
        fine = jnp.minimum(fine, jnp.where(seen, inside, 1.0))
        lse_ref[b:b + 1, :] = jnp.where(seen, jnp.log2(total), NEG)

    @pl.when(jnp.min(fine) < 0.5)
    def _():
        def block(b, c):
            m8[...] = jnp.full_like(m8, 0.5 * NEG)
            l8[0] = jnp.zeros((8, ROWS), F32)

            def tile(t, c):
                keys = ks[pl.ds(pl.multiple_of(t * KT, KT), KT), :]
                s = causal(nt(keys, q_all[b]) * C2, table, t, table.query_place(b), diff[...])
                s = s.reshape(KT // 8, 8, ROWS)
                m = m8[...]
                top = jnp.maximum(m, jnp.max(s, axis=0))
                l8[0] = l8[0] * jnp.exp2(m - top) + jnp.sum(jnp.exp2(s - top[None]), axis=0)
                m8[...] = top
                return c

            lax.fori_loop(0, (table.visible(b) + KB - 1) // KB, tile, 0)
            m = m8[...]
            top = jnp.max(m, axis=0, keepdims=True)
            total = jnp.sum(l8[0] * jnp.exp2(m - top), axis=0, keepdims=True)
            lse = jnp.where(table.visible(b) > 0, top + jnp.log2(total), NEG)
            lse_ref[pl.ds(b, 1), :] = lse
            shift_ref[pl.ds(b, 1), :] = lse
            return c

        lax.fori_loop(0, nq, block, 0)

        def entry(w, c):
            b, t, qp = table.entry(w)
            keys = ks[pl.ds(pl.multiple_of(t * KT, KT), KT), :]
            s = nt(keys, q_all[b]) * C2 - lse_ref[pl.ds(b, 1), :]
            e_buf[0, 0] = jnp.exp2(causal(s, table, t, qp, diff[...])).astype(BF16)
            place = e_ref.at[w // UNROLL, lax.rem(w, UNROLL)]
            copy = pltpu.make_async_copy(e_buf.at[0, 0], place, e_sem.at[0])
            copy.start()
            copy.wait()
            return c

        lax.fori_loop(1, table.end(), entry, 0)


def local_lse(table, pieces, columns):
    nq = 8
    count = 2 * columns[0].shape[0]
    nk = count // BLOCK
    row_shape = jax.ShapeDtypeStruct((count, DH), BF16)
    return pl.pallas_call(
        functools.partial(lse_kernel, nq, nk),
        out_shape=(
            jax.ShapeDtypeStruct((nq, ROWS), F32),
            jax.ShapeDtypeStruct((nq, ROWS), F32),
            jax.ShapeDtypeStruct((group_count(nq, nk), UNROLL, KT, ROWS), BF16),
            row_shape,
            row_shape,
            jax.ShapeDtypeStruct((DH, count), BF16),
        ),
        in_specs=[SMEM] + [VMEM] * 6,
        out_specs=(VMEM, VMEM, ANY) + (VMEM,) * 3,
        scratch_shapes=[
            pltpu.VMEM((nq, ROWS, DH), BF16),
            pltpu.VMEM((2, KT, ROWS), F32),
            pltpu.VMEM((BLOCK, ROWS), jnp.int32),
            pltpu.VMEM((nq, 8, ROWS), F32),
            pltpu.VMEM((8, ROWS), F32),
            pltpu.VMEM((DEPTH, UNROLL, KT, ROWS), BF16),
            pltpu.SemaphoreType.DMA((DEPTH,)),
        ],
        compiler_params=params(),
        cost_estimate=cost(1, nq, count),
        name="local_lse",
    )(table, *pieces, *columns)


def grad_kernel(nq, nk, table_ref, *refs):
    table = Table(table_ref, nq, nk)
    queries, grads, refs = refs[:4], refs[4:8], refs[8:]
    sums_in, (shift_ref, e_ref, ks, vs, kst), refs = refs[:4], refs[4:9], refs[9:]
    query_out, kv_out, kv_send, refs = refs[:5], refs[5], refs[6], refs[7:]
    q_all, g_all, factor, delta, sums, dqa, dp_buf, e_buf, e_sem = refs

    def fetch(i, slot):
        return pltpu.make_async_copy(e_ref.at[i], e_buf.at[slot], e_sem.at[slot])

    def fetch_body(i, slot):
        @pl.when(i < bodies(table.end()))
        def _():
            fetch(i, slot).start()

    for slot in range(DEPTH):
        fetch_body(slot, slot)
    for i in range(4):
        for j in range(2):
            b = 2 * i + j
            lse = combine([sums_in[d][b2:b2 + 1, :] for d in range(4) for b2 in [2 * ((i + d) % 4) + j]])
            factor[b] = jnp.exp2(shift_ref[b:b + 1, :] - lse)
            q_all[b] = queries[i][j]
            g_all[b] = grads[i][j, :ROWS, :]
            tail = grads[i][j, ROWS:, :].astype(F32)
            n = ROWS // DH
            tail = tail[0:n] + tail[n:2 * n] + tail[2 * n:3 * n]
            for c in range(n):
                delta[b, :, c * DH:(c + 1) * DH] = tail[c:c + 1]
    sums[...] = jnp.zeros_like(sums)
    dqa[...] = jnp.zeros_like(dqa)
    dp_buf[0] = jnp.zeros((KT, ROWS), F32)

    def prepare(w, slot):
        b, t, _ = table.entry(w)
        at = pl.ds(pl.multiple_of(t * KT, KT), KT)
        dp_buf[slot] = nt(vs[at, :], g_all[b])

    def use(w, slot, ring):
        b, t, _ = table.entry(w)
        at = pl.ds(pl.multiple_of(t * KT, KT), KT)
        p = e_buf[ring].astype(F32) * factor[b]
        ds = (p * (dp_buf[slot] - delta[b])).astype(BF16)
        sums[1, at, :] += nn(p.astype(BF16), g_all[b])
        sums[0, at, :] += nn(ds, q_all[b])
        dqa[b] += nn(kst[:, at], ds)

    run_work(
        table.end(),
        prepare,
        use,
        lambda i, slot: fetch(i, slot).wait(),
        lambda i, slot: fetch_body(i + DEPTH, slot),
    )
    for out, first in zip(query_out, (0, 2, 6, 4, 5)):
        for j in range(out.shape[0]):
            out[j] = (dqa[first + j] * SCALE).astype(out.dtype)

    for i, out in enumerate((kv_out, kv_send)):
        def body(j, c):
            r = pl.ds(pl.multiple_of(table.rank(i * nk // 2 + j) * BLOCK, BLOCK), BLOCK)
            at = pl.ds(pl.multiple_of(j * BLOCK, BLOCK), BLOCK)
            out[at, :DH] = (sums[0, r, :] * SCALE).astype(out.dtype)
            out[at, DH:] = sums[1, r, :].astype(out.dtype)
            return c

        lax.fori_loop(0, nk // 2, body, 0, unroll=2)


def local_grads(table, queries, grads, sums, results):
    nq = 8
    count = results[2].shape[0]
    nk = count // BLOCK
    return pl.pallas_call(
        functools.partial(grad_kernel, nq, nk),
        out_shape=tuple(jax.ShapeDtypeStruct((2, DH, ROWS), F32) for _ in range(3))
        + tuple(jax.ShapeDtypeStruct((1, DH, ROWS), BF16) for _ in range(2))
        + tuple(jax.ShapeDtypeStruct((count // 2, 2 * DH), t) for t in (F32, BF16)),
        in_specs=[SMEM] + [VMEM] * 13 + [ANY] + [VMEM] * 3,
        out_specs=(VMEM,) * 7,
        scratch_shapes=[
            pltpu.VMEM((nq, ROWS, DH), BF16),
            pltpu.VMEM((nq, ROWS, DH), BF16),
            pltpu.VMEM((nq, 1, ROWS), F32),
            pltpu.VMEM((nq, 1, ROWS), F32),
            pltpu.VMEM((2, count, DH), F32),
            pltpu.VMEM((nq, DH, ROWS), F32),
            pltpu.VMEM((2, KT, ROWS), F32),
            pltpu.VMEM((DEPTH, UNROLL, KT, ROWS), BF16),
            pltpu.SemaphoreType.DMA((DEPTH,)),
        ],
        compiler_params=params(),
        cost_estimate=cost(5, nq, count),
        name="local_grads",
    )(table, *queries, *grads, *sums, *results)


def along(axis, shift, size, array):
    return lax.ppermute(array, axis, [(i, (i + shift) % size) for i in range(size)])


def gather_y(own):
    one, three, two = (along("y", s, 4, own) for s in (1, 3, 2))
    return [own, one, two, three]


def shards(queries, keys, values, outputs, out_grad, block_order):
    x, zl, core, zh, y = (lax.axis_index(a) for a in ("x", "zl", "core", "zh", "y"))
    fence = lax.optimization_barrier

    pair = jnp.concatenate([keys, values], axis=1)
    column = lax.all_to_all(jnp.tile(pair, (16, 1)), KEY_AXES, 0, 0, tiled=True)
    columns = [column, along("core", 1, 2, column)]

    order = block_order.reshape(4, 2, 2, 2, 4, 2)
    key_place = lax.dynamic_slice(order, (0, 0, 0, 0, y, 0), (4, 2, 2, 2, 1, 2))
    key_place = jnp.moveaxis(key_place, 2, 0).reshape(2, 32)
    key_place = jnp.where(core == 0, key_place, key_place[::-1]).reshape(64)
    here = lax.dynamic_slice(order, (x, zl, core, zh, 0, 0), (1, 1, 1, 1, 4, 2)).reshape(4, 2)
    query_place = jnp.stack([here[(y - s) % 4] for s in range(4)]).reshape(8)
    rank = jnp.sum(key_place[:, None] < key_place[None, :], axis=0, dtype=jnp.int32)
    spots = lax.broadcasted_iota(jnp.int32, (64, 64), 0)
    place = jnp.sum(jnp.where(rank[None, :] == spots, key_place[None, :], 0), axis=1, dtype=jnp.int32)
    table = make_table(rank, place, query_place, key_place)

    query_message, grad_message = make_messages(queries, out_grad, outputs)
    query_pieces = gather_y(query_message)
    grad_pieces = gather_y(grad_message)

    (part, *results), grad_pieces[1:] = fence((local_lse(table, query_pieces, columns), grad_pieces[1:]))
    sums = [part] + [along("y", -d, 4, part) for d in (1, 2, 3)]

    own, one, three, two_a, two_b, kv_part, kv_send = local_grads(
        table, query_pieces, grad_pieces, sums, results
    )
    two_a, two_b = along("y", -1, 4, two_a), along("y", 1, 4, two_b)
    one = jnp.concatenate([one[:1] + two_a.astype(F32), one[1:]]).astype(BF16)
    three = jnp.concatenate([three[:1], three[1:] + two_b.astype(F32)]).astype(BF16)
    query_parts = [own, along("y", -1, 4, one), along("y", 1, 4, three)]
    kv_part = (kv_part + along("core", 1, 2, kv_send).astype(F32)).astype(BF16)
    terms = lax.all_to_all(kv_part, KEY_AXES, 0, 0, tiled=True)
    kv_grad = jnp.sum(terms.astype(F32).reshape(16, 2 * BLOCK, 2 * DH), axis=0)
    return finish_queries(query_parts), kv_grad[:, :DH], kv_grad[:, DH:]


def solution(mesh):
    fine = Mesh(mesh.devices.reshape(4, 2, 2, 2, 4), ("x", "zl", "core", "zh", "y"))
    rows = P(("x", "zl", "core", "zh", "y"), None)
    return jax.shard_map(
        shards,
        mesh=fine,
        in_specs=(rows,) * 5 + (P(),),
        out_specs=(rows,) * 3,
        check_vma=False,
    )
```

```python
import functools
import math

import jax
import jax.numpy as jnp
from jax import lax
from jax.experimental import pallas as pl
from jax.experimental.pallas import tpu as pltpu
from jax.sharding import Mesh, PartitionSpec as P

DH = 128
HEADS = 8
BLOCK = 64
ROWS = HEADS * BLOCK
GRAD_ROWS = ROWS + 16
DEPTH = 3
SCALE = DH ** -0.5
C2 = SCALE * math.log2(math.e)
NEG = -1e30
KB = 4
KT = KB * BLOCK
UNROLL = 8
VMEM_LIMIT = 56 * 1024 * 1024
F32 = jnp.float32
BF16 = jnp.bfloat16
KEY_AXES = ("x", "zl", "zh")
ANY = pl.BlockSpec(memory_space=pl.ANY)
SMEM = pl.BlockSpec(memory_space=pltpu.SMEM)
VMEM = pl.BlockSpec(memory_space=pltpu.VMEM)


def nn(a, b):
    return lax.dot_general(a, b, (((1,), (0,)), ((), ())), preferred_element_type=F32)


def nt(a, b):
    return lax.dot_general(a, b, (((1,), (1,)), ((), ())), preferred_element_type=F32)


def params():
    return pltpu.CompilerParams(vmem_limit_bytes=VMEM_LIMIT)


def cost(products, nq, count):
    area = nq * ROWS * count // 2
    return pl.CostEstimate(flops=products * 4 * area * DH, bytes_accessed=8 << 20, transcendentals=area)


def message_kernel(q_ref, g_ref, o_ref, query_ref, grad_ref):
    for blk in range(2):
        tokens = slice(blk * BLOCK, (blk + 1) * BLOCK)
        parts = []
        for h in range(HEADS):
            lanes = slice(h * DH, (h + 1) * DH)
            g = g_ref[tokens, lanes]
            query_ref[blk, h * BLOCK:(h + 1) * BLOCK, :] = q_ref[tokens, lanes]
            grad_ref[blk, h * BLOCK:(h + 1) * BLOCK, :] = g
            parts.append(g.astype(F32) * o_ref[tokens, lanes].astype(F32))
        delta = jnp.sum(jnp.concatenate(parts, 0).T, axis=0, keepdims=True)
        rows = []
        rest = delta
        for _ in range(3):
            part = rest.astype(BF16).astype(F32)
            rest = rest - part
            rows += [part[:, c * DH:(c + 1) * DH] for c in range(ROWS // DH)]
        rows.append(jnp.zeros((16 - len(rows), DH), F32))
        grad_ref[blk, ROWS:, :] = jnp.concatenate(rows, 0).astype(BF16)


def make_messages(queries, out_grad, outputs):
    return pl.pallas_call(
        message_kernel,
        out_shape=(
            jax.ShapeDtypeStruct((2, ROWS, DH), BF16),
            jax.ShapeDtypeStruct((2, GRAD_ROWS, DH), BF16),
        ),
        in_specs=[VMEM] * 3,
        out_specs=(VMEM,) * 2,
        compiler_params=params(),
        name="make_messages",
    )(queries, out_grad, outputs)


def finish_kernel(*refs):
    out_ref = refs[-1]
    for blk in range(2):
        total = refs[0][blk]
        for other in refs[1:3]:
            total = total + other[blk].astype(F32)
        total = total.T.astype(BF16)
        for h in range(HEADS):
            out_ref[blk * BLOCK:(blk + 1) * BLOCK, h * DH:(h + 1) * DH] = total[h * BLOCK:(h + 1) * BLOCK]


def finish_queries(parts):
    return pl.pallas_call(
        finish_kernel,
        out_shape=jax.ShapeDtypeStruct((2 * BLOCK, HEADS * DH), BF16),
        in_specs=[VMEM] * 3,
        out_specs=VMEM,
        compiler_params=params(),
        name="finish_queries",
    )(*parts)


def sort_blocks(table, src, lanes, dst, start, nk):
    def body(j, c):
        r = pl.multiple_of(table.rank(start + j) * BLOCK, BLOCK)
        dst[pl.ds(r, BLOCK), :] = src[pl.ds(pl.multiple_of(j * BLOCK, BLOCK), BLOCK), lanes]
        return c

    lax.fori_loop(0, nk, body, 0, unroll=4)


class Table:
    def __init__(self, ref, nq, nk):
        size = list_size(nq, nk)
        starts = [0]
        for n in (nk, nk, nq, nq, size, size, size, 1):
            starts.append(starts[-1] + n)
        self.ref, self.starts = ref, starts

    def rank(self, j):
        return self.ref[self.starts[0] + j]

    def place(self, j):
        return self.ref[self.starts[1] + j]

    def visible(self, b):
        return self.ref[self.starts[2] + b]

    def query_place(self, b):
        return self.ref[self.starts[3] + b]

    def entry(self, w):
        return tuple(self.ref[self.starts[i] + w] for i in (4, 5, 6))

    def end(self):
        return self.ref[self.starts[7]]


def list_size(nq, nk):
    most = nq * ((nk + KB - 1) // KB) + 1
    return (most + UNROLL - 1) // UNROLL * UNROLL + 1


def group_count(nq, nk):
    return list_size(nq, nk) // UNROLL


def make_table(rank, place, query_place, key_place):
    nq, nk = query_place.shape[0], key_place.shape[0]
    visible = jnp.sum(key_place[None, :] <= query_place[:, None], axis=1, dtype=jnp.int32)
    count = (visible + KB - 1) // KB
    earlier = jnp.arange(nq)[:, None] > jnp.arange(nq)[None, :]
    start = jnp.sum(jnp.where(earlier, count[None, :], 0), axis=1, dtype=jnp.int32) + 1
    w = jnp.arange(list_size(nq, nk), dtype=jnp.int32)[:, None]
    inside = (w >= start[None, :]) & (w < (start + count)[None, :])

    def pick(a):
        return jnp.sum(jnp.where(inside, a, 0), axis=1, dtype=jnp.int32)

    ids = jnp.arange(nq, dtype=jnp.int32)[None, :]
    lists = [pick(ids), pick(w - start[None, :]), pick(query_place[None, :] + 1) - 1]
    end = jnp.sum(count, dtype=jnp.int32).reshape(1) + 1
    return jnp.concatenate([rank, place, visible, query_place, *lists, end])


def run_work(end, prepare, use, before, after):
    def body(i, c):
        slot = lax.rem(i, DEPTH)
        before(i, slot)
        for u in range(UNROLL):
            prepare(i * UNROLL + u + 1, (u + 1) % 2)
            use(i * UNROLL + u, u % 2, (slot, u))
        after(i, slot)
        return c

    whole = end // UNROLL
    lax.fori_loop(0, whole, body, 0)
    rest = end - whole * UNROLL

    @pl.when(rest > 0)
    def _():
        slot = lax.rem(whole, DEPTH)
        before(whole, slot)

        def pair(i, c):
            for u in range(2):
                w = whole * UNROLL + 2 * i + u
                prepare(w + 1, (u + 1) % 2)
                use(w, u % 2, (slot, 2 * i + u))
            return c

        lax.fori_loop(0, (rest + 1) // 2, pair, 0)
        after(whole, slot)


def bodies(end):
    return (end + UNROLL - 1) // UNROLL


def difference():
    key = lax.broadcasted_iota(jnp.int32, (BLOCK, ROWS), 0)
    query = lax.broadcasted_iota(jnp.int32, (BLOCK, ROWS), 1) % BLOCK
    return key - query


def causal(s, table, t, query_place, diff):
    parts = []
    for u in range(KB):
        place = table.place(t * KB + u)
        limit = jnp.where(place < query_place, BLOCK, jnp.where(place == query_place, 0, -2 * BLOCK))
        parts.append(jnp.where(diff <= limit, s[u * BLOCK:(u + 1) * BLOCK], NEG))
    return jnp.concatenate(parts, 0)


def combine(parts):
    top = functools.reduce(jnp.maximum, parts)
    return top + jnp.log2(sum(jnp.exp2(part - top) for part in parts))


def lse_kernel(nq, nk, table_ref, *refs):
    table = Table(table_ref, nq, nk)
    pieces, columns, refs = refs[:4], refs[4:6], refs[6:]
    lse_ref, shift_ref, e_ref, ks, vs, kst, q_all, s_buf, diff, l8, m8, e_buf, e_sem = refs
    for i, column in enumerate(columns):
        sort_blocks(table, column, slice(0, DH), ks, i * nk // 2, nk // 2)
        sort_blocks(table, column, slice(DH, 2 * DH), vs, i * nk // 2, nk // 2)
    kst[...] = ks[...].T
    for i, piece in enumerate(pieces):
        q_all[2 * i:2 * i + 2] = piece[...]
    diff[...] = difference()
    l8[...] = jnp.zeros_like(l8)

    def send(i, slot):
        return pltpu.make_async_copy(e_buf.at[slot], e_ref.at[i], e_sem.at[slot])

    def free(i, slot):
        @pl.when(i >= DEPTH)
        def _():
            send(i, slot).wait()

    def prepare(w, slot):
        b, t, _ = table.entry(w)
        keys = ks[pl.ds(pl.multiple_of(t * KT, KT), KT), :]
        s_buf[slot] = nt(keys, q_all[b])

    def use(w, slot, ring):
        b, t, qp = table.entry(w)
        e = jnp.exp2(causal(s_buf[slot] * C2, table, t, qp, diff[...]))
        l8[b] += jnp.sum(e.reshape(KT // 8, 8, ROWS), axis=0)
        e_buf[ring] = e.astype(BF16)

    run_work(
        table.end(), prepare, use, free, lambda i, slot: send(i, slot).start()
    )
    for slot in range(DEPTH):

        @pl.when(slot < bodies(table.end()))
        def _():
            send(slot, slot).wait()

    shift_ref[...] = jnp.zeros_like(shift_ref)
    fine = jnp.ones((1, ROWS), F32)
    for b in range(nq):
        total = jnp.sum(l8[b], axis=0, keepdims=True)
        seen = table.visible(b) > 0
        inside = jnp.where((total > 1e-18) & (total < 1e30), 1.0, 0.0)
        fine = jnp.minimum(fine, jnp.where(seen, inside, 1.0))
        lse_ref[b:b + 1, :] = jnp.where(seen, jnp.log2(total), NEG)

    @pl.when(jnp.min(fine) < 0.5)
    def _():
        def block(b, c):
            m8[...] = jnp.full_like(m8, 0.5 * NEG)
            l8[0] = jnp.zeros((8, ROWS), F32)

            def tile(t, c):
                keys = ks[pl.ds(pl.multiple_of(t * KT, KT), KT), :]
                s = causal(nt(keys, q_all[b]) * C2, table, t, table.query_place(b), diff[...])
                s = s.reshape(KT // 8, 8, ROWS)
                m = m8[...]
                top = jnp.maximum(m, jnp.max(s, axis=0))
                l8[0] = l8[0] * jnp.exp2(m - top) + jnp.sum(jnp.exp2(s - top[None]), axis=0)
                m8[...] = top
                return c

            lax.fori_loop(0, (table.visible(b) + KB - 1) // KB, tile, 0)
            m = m8[...]
            top = jnp.max(m, axis=0, keepdims=True)
            total = jnp.sum(l8[0] * jnp.exp2(m - top), axis=0, keepdims=True)
            lse = jnp.where(table.visible(b) > 0, top + jnp.log2(total), NEG)
            lse_ref[pl.ds(b, 1), :] = lse
            shift_ref[pl.ds(b, 1), :] = lse
            return c

        lax.fori_loop(0, nq, block, 0)

        def entry(w, c):
            b, t, qp = table.entry(w)
            keys = ks[pl.ds(pl.multiple_of(t * KT, KT), KT), :]
            s = nt(keys, q_all[b]) * C2 - lse_ref[pl.ds(b, 1), :]
            e_buf[0, 0] = jnp.exp2(causal(s, table, t, qp, diff[...])).astype(BF16)
            place = e_ref.at[w // UNROLL, lax.rem(w, UNROLL)]
            copy = pltpu.make_async_copy(e_buf.at[0, 0], place, e_sem.at[0])
            copy.start()
            copy.wait()
            return c

        lax.fori_loop(1, table.end(), entry, 0)


def local_lse(table, pieces, columns):
    nq = 8
    count = 2 * columns[0].shape[0]
    nk = count // BLOCK
    row_shape = jax.ShapeDtypeStruct((count, DH), BF16)
    return pl.pallas_call(
        functools.partial(lse_kernel, nq, nk),
        out_shape=(
            jax.ShapeDtypeStruct((nq, ROWS), F32),
            jax.ShapeDtypeStruct((nq, ROWS), F32),
            jax.ShapeDtypeStruct((group_count(nq, nk), UNROLL, KT, ROWS), BF16),
            row_shape,
            row_shape,
            jax.ShapeDtypeStruct((DH, count), BF16),
        ),
        in_specs=[SMEM] + [VMEM] * 6,
        out_specs=(VMEM, VMEM, ANY) + (VMEM,) * 3,
        scratch_shapes=[
            pltpu.VMEM((nq, ROWS, DH), BF16),
            pltpu.VMEM((2, KT, ROWS), F32),
            pltpu.VMEM((BLOCK, ROWS), jnp.int32),
            pltpu.VMEM((nq, 8, ROWS), F32),
            pltpu.VMEM((8, ROWS), F32),
            pltpu.VMEM((DEPTH, UNROLL, KT, ROWS), BF16),
            pltpu.SemaphoreType.DMA((DEPTH,)),
        ],
        compiler_params=params(),
        cost_estimate=cost(1, nq, count),
        name="local_lse",
    )(table, *pieces, *columns)


def grad_kernel(nq, nk, table_ref, *refs):
    table = Table(table_ref, nq, nk)
    queries, grads, refs = refs[:4], refs[4:8], refs[8:]
    sums_in, (shift_ref, e_ref, ks, vs, kst), refs = refs[:4], refs[4:9], refs[9:]
    query_out, kv_out, kv_send, refs = refs[:5], refs[5], refs[6], refs[7:]
    q_all, g_all, factor, delta, sums, dqa, dp_buf, e_buf, e_sem = refs

    def fetch(i, slot):
        return pltpu.make_async_copy(e_ref.at[i], e_buf.at[slot], e_sem.at[slot])

    def fetch_body(i, slot):
        @pl.when(i < bodies(table.end()))
        def _():
            fetch(i, slot).start()

    for slot in range(DEPTH):
        fetch_body(slot, slot)
    for i in range(4):
        for j in range(2):
            b = 2 * i + j
            lse = combine([sums_in[d][b2:b2 + 1, :] for d in range(4) for b2 in [2 * ((i + d) % 4) + j]])
            factor[b] = jnp.exp2(shift_ref[b:b + 1, :] - lse)
            q_all[b] = queries[i][j]
            g_all[b] = grads[i][j, :ROWS, :]
            tail = grads[i][j, ROWS:, :].astype(F32)
            n = ROWS // DH
            tail = tail[0:n] + tail[n:2 * n] + tail[2 * n:3 * n]
            for c in range(n):
                delta[b, :, c * DH:(c + 1) * DH] = tail[c:c + 1]
    sums[...] = jnp.zeros_like(sums)
    dqa[...] = jnp.zeros_like(dqa)
    dp_buf[0] = jnp.zeros((KT, ROWS), F32)

    def prepare(w, slot):
        b, t, _ = table.entry(w)
        at = pl.ds(pl.multiple_of(t * KT, KT), KT)
        dp_buf[slot] = nt(vs[at, :], g_all[b])

    def use(w, slot, ring):
        b, t, _ = table.entry(w)
        at = pl.ds(pl.multiple_of(t * KT, KT), KT)
        p = e_buf[ring].astype(F32) * factor[b]
        ds = (p * (dp_buf[slot] - delta[b])).astype(BF16)
        sums[1, at, :] += nn(p.astype(BF16), g_all[b])
        sums[0, at, :] += nn(ds, q_all[b])
        dqa[b] += nn(kst[:, at], ds)

    run_work(
        table.end(),
        prepare,
        use,
        lambda i, slot: fetch(i, slot).wait(),
        lambda i, slot: fetch_body(i + DEPTH, slot),
    )
    for out, first in zip(query_out, (0, 2, 6, 4, 5)):
        for j in range(out.shape[0]):
            out[j] = (dqa[first + j] * SCALE).astype(out.dtype)

    for i, out in enumerate((kv_out, kv_send)):
        def body(j, c):
            r = pl.ds(pl.multiple_of(table.rank(i * nk // 2 + j) * BLOCK, BLOCK), BLOCK)
            at = pl.ds(pl.multiple_of(j * BLOCK, BLOCK), BLOCK)
            out[at, :DH] = (sums[0, r, :] * SCALE).astype(out.dtype)
            out[at, DH:] = sums[1, r, :].astype(out.dtype)
            return c

        lax.fori_loop(0, nk // 2, body, 0, unroll=2)


def local_grads(table, queries, grads, sums, results):
    nq = 8
    count = results[2].shape[0]
    nk = count // BLOCK
    return pl.pallas_call(
        functools.partial(grad_kernel, nq, nk),
        out_shape=tuple(jax.ShapeDtypeStruct((2, DH, ROWS), F32) for _ in range(3))
        + tuple(jax.ShapeDtypeStruct((1, DH, ROWS), BF16) for _ in range(2))
        + tuple(jax.ShapeDtypeStruct((count // 2, 2 * DH), t) for t in (F32, BF16)),
        in_specs=[SMEM] + [VMEM] * 13 + [ANY] + [VMEM] * 3,
        out_specs=(VMEM,) * 7,
        scratch_shapes=[
            pltpu.VMEM((nq, ROWS, DH), BF16),
            pltpu.VMEM((nq, ROWS, DH), BF16),
            pltpu.VMEM((nq, 1, ROWS), F32),
            pltpu.VMEM((nq, 1, ROWS), F32),
            pltpu.VMEM((2, count, DH), F32),
            pltpu.VMEM((nq, DH, ROWS), F32),
            pltpu.VMEM((2, KT, ROWS), F32),
            pltpu.VMEM((DEPTH, UNROLL, KT, ROWS), BF16),
            pltpu.SemaphoreType.DMA((DEPTH,)),
        ],
        compiler_params=params(),
        cost_estimate=cost(5, nq, count),
        name="local_grads",
    )(table, *queries, *grads, *sums, *results)


def along(axis, shift, size, array):
    return lax.ppermute(array, axis, [(i, (i + shift) % size) for i in range(size)])


def gather_y(own):
    one, three, two = (along("y", s, 4, own) for s in (1, 3, 2))
    return [own, one, two, three]


def shards(queries, keys, values, outputs, out_grad, block_order):
    x, zl, core, zh, y = (lax.axis_index(a) for a in ("x", "zl", "core", "zh", "y"))
    fence = lax.optimization_barrier

    pair = jnp.concatenate([keys, values], axis=1)
    column = lax.all_to_all(jnp.tile(pair, (16, 1)), KEY_AXES, 0, 0, tiled=True)
    columns = [column, along("core", 1, 2, column)]

    order = block_order.reshape(4, 2, 2, 2, 4, 2)
    key_place = lax.dynamic_slice(order, (0, 0, 0, 0, y, 0), (4, 2, 2, 2, 1, 2))
    key_place = jnp.moveaxis(key_place, 2, 0).reshape(2, 32)
    key_place = jnp.where(core == 0, key_place, key_place[::-1]).reshape(64)
    here = lax.dynamic_slice(order, (x, zl, core, zh, 0, 0), (1, 1, 1, 1, 4, 2)).reshape(4, 2)
    query_place = jnp.stack([here[(y - s) % 4] for s in range(4)]).reshape(8)
    rank = jnp.sum(key_place[:, None] < key_place[None, :], axis=0, dtype=jnp.int32)
    spots = lax.broadcasted_iota(jnp.int32, (64, 64), 0)
    place = jnp.sum(jnp.where(rank[None, :] == spots, key_place[None, :], 0), axis=1, dtype=jnp.int32)
    table = make_table(rank, place, query_place, key_place)

    query_message, grad_message = make_messages(queries, out_grad, outputs)
    query_pieces = gather_y(query_message)
    grad_pieces = gather_y(grad_message)

    (part, *results), grad_pieces[1:] = fence((local_lse(table, query_pieces, columns), grad_pieces[1:]))
    sums = [part] + [along("y", -d, 4, part) for d in (1, 2, 3)]

    own, one, three, two_a, two_b, kv_part, kv_send = local_grads(
        table, query_pieces, grad_pieces, sums, results
    )
    two_a, two_b = along("y", -1, 4, two_a), along("y", 1, 4, two_b)
    one = jnp.concatenate([one[:1] + two_a.astype(F32), one[1:]]).astype(BF16)
    three = jnp.concatenate([three[:1], three[1:] + two_b.astype(F32)]).astype(BF16)
    query_parts = [own, along("y", -1, 4, one), along("y", 1, 4, three)]
    kv_part = (kv_part + along("core", 1, 2, kv_send).astype(F32)).astype(BF16)
    terms = lax.all_to_all(kv_part, KEY_AXES, 0, 0, tiled=True)
    kv_grad = jnp.sum(terms.astype(F32).reshape(16, 2 * BLOCK, 2 * DH), axis=0)
    kv_grad, query_parts[0] = fence((kv_grad, query_parts[0]))
    return finish_queries(query_parts), kv_grad[:, :DH], kv_grad[:, DH:]


def solution(mesh):
    fine = Mesh(mesh.devices.reshape(4, 2, 2, 2, 4), ("x", "zl", "core", "zh", "y"))
    rows = P(("x", "zl", "core", "zh", "y"), None)
    return jax.shard_map(
        shards,
        mesh=fine,
        in_specs=(rows,) * 5 + (P(),),
        out_specs=(rows,) * 3,
        check_vma=False,
    )
```
